32 devices in a mesh: row: 4 (over x, core), col: 8 (over z, y).
Axes of the slice: x: 2, y: 2, z: 4, core: 2. Of those that a mesh axis runs over, the one named last changes fastest.
Arguments:
- row_points: bfloat16 [64, 64, 256], P('row'), may hold values from -25.5 to 25.5
- col_points: bfloat16 [32, 64, 256], P('col'), may hold values from -25.5 to 25.5
- block_lists: int32 [64, 16], P('row'), may hold values from 0 to 31, as said below
Outputs:
- row_potential: float32 [64, 256], P('row')
- col_potential: float32 [32, 256], P('col')
The draws below stay inside these ranges and needn't reach their ends.
Inputs may be any that keep to these rules, and one draw needn't show every extreme that they name: `block_lists`: the 16 column blocks of a row block are distinct. Among the row blocks of one index of row, at most 64 list entries name column blocks of one index of col, and exactly 64 for some index of col. Every column block is named by some row block of every index of row.
All inputs are finite; a program needn't handle non-finite values.
Results may differ from the reference program's by a relative error of at most 0.0003.
Values sent between devices are 32-bit elements; how exact they have to be, the bound alone decides.
A program may use at most 64 MiB of HBM per device.

```python
import math
import jax
import jax.numpy as jnp
from jax import lax

BLOCK = 256
DIM = 64
LIST = 16
ITERS = 4
PAIR_MEAN = 32
COL_BLOCKS_DEV = 4
ROW_BLOCKS_DEV = 16
ROW_BLOCKS = 64
COL_BLOCKS = 32
N_ROW = 4
N_COL = 8


def point_cloud(key, blocks):
    subkeys = jax.random.split(key, 1)
    full_shape = (blocks, DIM, BLOCK)
    values = jnp.clip(jax.random.normal(subkeys[0], full_shape, jnp.float32), -4.0, 4.0)
    return values.astype(jnp.bfloat16)


def draw_row_points(key, part):
    return point_cloud(jax.random.fold_in(key, 11), ROW_BLOCKS)


def draw_col_points(key, part):
    return point_cloud(jax.random.fold_in(key, 23), COL_BLOCKS)


def shard_lists(shard_key):
    subkeys = jax.random.split(shard_key, 3)
    shuffle = jax.random.permutation(subkeys[0], N_COL)
    rank_list = jnp.arange(N_COL, dtype=jnp.int32)
    half_mean = PAIR_MEAN // 2
    spreads = jax.random.randint(subkeys[1], (N_COL,), 0, half_mean - COL_BLOCKS_DEV + 1, dtype=jnp.int32)
    offset_rank = rank_list - 3
    pair_index = jnp.maximum(offset_rank, 0) // 2
    sign_vals = jnp.where(offset_rank % 2 == 0, 1, -1).astype(jnp.int32)
    has_partner = (offset_rank % 2 == 1) | (rank_list + 1 < N_COL)
    paired = sign_vals * spreads[pair_index] * has_partner.astype(jnp.int32)
    adjust = jnp.where(rank_list == 0, PAIR_MEAN, jnp.where(rank_list < 3, -half_mean, paired)).astype(jnp.int32)
    counts = jnp.zeros((N_COL,), jnp.int32).at[shuffle].set(PAIR_MEAN + adjust)
    run_ends = jnp.cumsum(counts)
    starts = run_ends - counts
    positions = jnp.arange(LIST * ROW_BLOCKS_DEV, dtype=jnp.int32)
    device = jnp.sum((run_ends[None, :] <= positions[:, None]).astype(jnp.int32), axis=1)
    within = positions - starts[device]
    offsets = jax.random.randint(subkeys[2], (N_COL,), 0, COL_BLOCKS_DEV, dtype=jnp.int32)
    local_id = (offsets[device] + within + within // ROW_BLOCKS_DEV) % COL_BLOCKS_DEV
    block_ids = device * COL_BLOCKS_DEV + local_id
    return block_ids.reshape(LIST, ROW_BLOCKS_DEV).T


def draw_block_lists(key, part):
    shard_keys = jax.random.split(jax.random.fold_in(key, 37), N_ROW)
    return jax.vmap(shard_lists)(shard_keys).reshape(ROW_BLOCKS, LIST).astype(jnp.int32)


def setup_inputs(seed: int = 0) -> dict:
    splits = jax.random.split(jax.random.key(seed), 4)
    return {
        "row_points": draw_row_points(jax.random.fold_in(splits[3], 71), 0),
        "col_points": draw_col_points(jax.random.fold_in(splits[3], 71), 0),
        "block_lists": draw_block_lists(jax.random.fold_in(splits[3], 71), 0),
    }


eps_reg = 0.05
neg_big = -1.0e30


def cost_tiles(row_tile, row_norm, col_tiles, col_norms):
    inner_prod = jnp.einsum("dp,kdq->kpq", row_tile.astype(jnp.float32), col_tiles.astype(jnp.float32), precision=lax.Precision.HIGHEST)
    return (row_norm[None, :, None] + col_norms[:, None, :] - 2.0 * inner_prod) / DIM


def reference(row_points, col_points, block_lists):
    row_norms = jnp.sum(jnp.square(row_points.astype(jnp.float32)), axis=1)
    col_norms = jnp.sum(jnp.square(col_points.astype(jnp.float32)), axis=1)
    row_mass = -math.log(ROW_BLOCKS * BLOCK)
    col_mass = -math.log(COL_BLOCKS * BLOCK)
    flat_ids = block_lists.reshape(-1).astype(jnp.int32)
    col_potential = jnp.zeros((COL_BLOCKS, BLOCK), jnp.float32)
    row_potential = jnp.zeros((ROW_BLOCKS, BLOCK), jnp.float32)
    for sweep in range(ITERS):
        def row_update(members):
            row_tile, row_norm, listed = members
            tiles = cost_tiles(row_tile, row_norm, col_points[listed], col_norms[listed])
            scores = (col_potential[listed][:, None, :] - tiles) / eps_reg
            peak_vals = jnp.max(scores, axis=(0, 2))
            totals = jnp.sum(jnp.exp(scores - peak_vals[None, :, None]), axis=(0, 2))
            return eps_reg * (row_mass - (peak_vals + jnp.log(totals)))

        row_potential = lax.map(row_update, (row_points, row_norms, block_lists))

        def col_partials(members):
            row_tile, row_norm, row_pot, listed = members
            tiles = cost_tiles(row_tile, row_norm, col_points[listed], col_norms[listed])
            scores = (row_pot[None, :, None] - tiles) / eps_reg
            peak_vals = jnp.max(scores, axis=1)
            totals = jnp.sum(jnp.exp(scores - peak_vals[:, None, :]), axis=1)
            return peak_vals, totals

        peak_parts, partial_sums = lax.map(col_partials, (row_points, row_norms, row_potential, block_lists))
        peak_parts = peak_parts.reshape(-1, BLOCK)
        partial_sums = partial_sums.reshape(-1, BLOCK)
        block_peak = jnp.full((COL_BLOCKS, BLOCK), neg_big, jnp.float32).at[flat_ids].max(peak_parts)
        scaled = partial_sums * jnp.exp(peak_parts - block_peak[flat_ids])
        block_sum = jnp.zeros((COL_BLOCKS, BLOCK), jnp.float32).at[flat_ids].add(scaled)
        col_potential = eps_reg * (col_mass - (block_peak + jnp.log(block_sum)))
    return row_potential, col_potential
```

```python
import functools
import math

import jax
import jax.numpy as jnp
from jax import lax
from jax.experimental import pallas as pl
from jax.experimental.pallas import tpu as pltpu
from jax.sharding import PartitionSpec as P

ITERS = 4
eps_reg = 0.05
kappa = math.log2(math.e) / eps_reg
masked_score = -(2.0**40)
depth = 256
slab = 16
MESH = pl.DeviceIdType.MESH


def split3(values):
    high = values.astype(jnp.bfloat16).astype(jnp.float32)
    rest = values - high
    mid = rest.astype(jnp.bfloat16).astype(jnp.float32)
    low = (rest - mid).astype(jnp.bfloat16).astype(jnp.float32)
    return high, mid, low


def with_bias(base, bias, first):
    rows = lax.broadcasted_iota(jnp.int32, base.shape, 0)
    high, mid, low = split3(bias)
    out = jnp.where(rows == first, high, base)
    out = jnp.where(rows == first + 1, mid, out)
    return jnp.where(rows == first + 2, low, out)


def log2_sum(parts):
    peak = jnp.max(parts, axis=0, keepdims=True)
    return peak + jnp.log2(jnp.sum(jnp.exp2(parts - peak), axis=0, keepdims=True))


def kernel(
    n_row, n_col, lists_ref, x_ref, y_ref, f_ref, g_ref,
    a_ref, at_ref, b_ref, bt_ref, abase, bbase, t_ref, u_ref, nx_ref, ny_ref,
    l_ref, rs_recv, lc_ref, c_send, c_recv, s_ref,
    rs_ssem, rs_rsem, ag_ssem, ag_rsem, c_ssem, c_rsem,
):
    me_row = lax.axis_index("row")
    me_col = lax.axis_index("col")
    row_blocks, dim, block = x_ref.shape
    col_blocks = y_ref.shape[0]
    per = row_blocks // n_col
    width = per * block
    cols = col_blocks * block
    log2_a = -math.log2(n_row * row_blocks * block)
    log2_b = -math.log2(n_col * cols)
    alpha = 2.0 * kappa / dim
    beta = kappa / dim

    barrier = pltpu.get_barrier_semaphore()
    for step in range(1, n_col):
        pl.semaphore_signal(
            barrier, inc=1, device_id={"col": lax.rem(me_col + step, n_col)}, device_id_type=MESH
        )
    for step in range(1, n_row):
        pl.semaphore_signal(
            barrier, inc=1, device_id={"row": lax.rem(me_row + step, n_row)}, device_id_type=MESH
        )

    slab_rows = lax.broadcasted_iota(jnp.int32, (slab, block), 0)
    zeros = jnp.zeros((depth - 3 * dim - slab, block), jnp.bfloat16)

    for c in range(col_blocks):
        lanes = pl.ds(c * block, block)
        y = y_ref[c]
        for part in range(3):
            b_ref[pl.ds(part * dim, dim), lanes] = y
        y32 = y.astype(jnp.float32)
        norm = jnp.sum(y32 * y32, axis=0, keepdims=True) * beta
        ny_ref[:, lanes] = norm
        u_ref[:, lanes] = -norm
        base = jnp.where((slab_rows < 3) | (slab_rows == 6 + c), 1.0, 0.0)
        bbase[:, lanes] = base
        b_ref[pl.ds(3 * dim, slab), lanes] = with_bias(base, -norm, 3).astype(jnp.bfloat16)
        b_ref[pl.ds(3 * dim + slab, depth - 3 * dim - slab), lanes] = zeros
        bt_ref[pl.ds(c * block, block), :] = b_ref[:, lanes].T

    def prepare(q, carry):
        for part in range(per):
            r = q * per + part
            lanes = pl.ds(part * block, block)
            x = x_ref[r].astype(jnp.float32)
            norm = jnp.sum(x * x, axis=0, keepdims=True) * beta
            nx_ref[q, :, lanes] = norm
            t_ref[q, :, lanes] = -norm
            for i, piece in enumerate(split3(x * alpha)):
                a_ref[q, pl.ds(i * dim, dim), lanes] = piece.astype(jnp.bfloat16)
            listed = lists_ref[pl.ds(r, 1), :]
            base = jnp.where((slab_rows >= 3) & (slab_rows < 6), 1.0, 0.0)
            for c in range(col_blocks):
                hit = jnp.where(listed == me_col * col_blocks + c, 1.0, 0.0)
                hit = jnp.max(hit, axis=1, keepdims=True)
                fill = jnp.broadcast_to(jnp.where(hit > 0.0, 0.0, masked_score), (slab, block))
                base = jnp.where(slab_rows == 6 + c, fill, base)
            abase[q, :, lanes] = base
            a_ref[q, pl.ds(3 * dim, slab), lanes] = with_bias(base, -norm, 0).astype(jnp.bfloat16)
            a_ref[q, pl.ds(3 * dim + slab, depth - 3 * dim - slab), lanes] = zeros
            at_ref[q, pl.ds(part * block, block), :] = a_ref[q, :, lanes].T
        return carry

    lax.fori_loop(0, n_col, prepare, 0)
    pl.semaphore_wait(barrier, n_col - 1 + n_row - 1)

    def row_part(q):
        points = a_ref[q]
        peak = None
        for c in range(col_blocks):
            scores = jnp.dot(
                bt_ref[pl.ds(c * block, block), :], points, preferred_element_type=jnp.float32
            )
            s_ref[c] = scores
            top = jnp.max(scores.reshape(block // 8, 8, width), axis=0)
            peak = top if peak is None else jnp.maximum(peak, top)
        peak = jnp.max(peak, axis=0, keepdims=True)
        total = jnp.zeros((8, width), jnp.float32)
        for c in range(col_blocks):
            total += jnp.sum(jnp.exp2(s_ref[c] - peak).reshape(block // 8, 8, width), axis=0)
        return peak + jnp.log2(jnp.sum(total, axis=0, keepdims=True))

    def scatter_copy(peer, slot):
        return pltpu.make_async_remote_copy(
            src_ref=l_ref.at[peer], dst_ref=rs_recv.at[slot],
            send_sem=rs_ssem.at[peer], recv_sem=rs_rsem.at[slot],
            device_id={"col": peer}, device_id_type=MESH,
        )

    def gather_copy(peer, slot):
        return pltpu.make_async_remote_copy(
            src_ref=t_ref.at[slot], dst_ref=t_ref.at[slot],
            send_sem=ag_ssem.at[peer], recv_sem=ag_rsem.at[slot],
            device_id={"col": peer}, device_id_type=MESH,
        )

    def col_copy(peer, slot, k):
        return pltpu.make_async_remote_copy(
            src_ref=c_send.at[k], dst_ref=c_recv.at[k, slot],
            send_sem=c_ssem.at[k, peer], recv_sem=c_rsem.at[k, slot],
            device_id={"row": peer}, device_id_type=MESH,
        )

    def iteration(k, carry):
        def row_step(s, c2):
            q = lax.rem(me_col + 1 + s, n_col)
            l_ref[q] = row_part(q)

            @pl.when(s < n_col - 1)
            def _():
                scatter_copy(q, me_col).start()

            return c2

        lax.fori_loop(0, n_col, row_step, 0)
        rs_recv[me_col] = l_ref[me_col]

        def row_wait(s, c2):
            scatter_copy(me_col, lax.rem(me_col + 1 + s, n_col)).wait_recv()
            return c2

        lax.fori_loop(0, n_col - 1, row_wait, 0)
        whole = log2_sum(rs_recv[...])
        t_ref[me_col] = t_ref[me_col] + (log2_a - whole[0])

        def row_send(s, c2):
            gather_copy(lax.rem(me_col + 1 + s, n_col), me_col).start()
            return c2

        lax.fori_loop(0, n_col - 1, row_send, 0)

        def col_step(s, c2):
            q = lax.rem(me_col + s, n_col)

            @pl.when(s > 0)
            def _():
                gather_copy(me_col, q).wait_recv()

            a_ref[q, pl.ds(3 * dim, slab), :] = with_bias(abase[q], t_ref[q], 0).astype(
                jnp.bfloat16
            )
            at_ref[q, :, pl.ds(depth // 2, depth // 2)] = a_ref[
                q, pl.ds(depth // 2, depth // 2), :
            ].T
            points = at_ref[q]
            for c in range(col_blocks):
                lanes = pl.ds(c * block, block)
                scores = jnp.dot(points, b_ref[:, lanes], preferred_element_type=jnp.float32)
                peak = jnp.max(scores, axis=0, keepdims=True)
                total = jnp.sum(jnp.exp2(scores - peak), axis=0, keepdims=True)
                lc_ref[q, :, lanes] = peak + jnp.log2(total)
            return c2

        lax.fori_loop(0, n_col, col_step, 0)
        c_send[k] = log2_sum(lc_ref[...])[0]

        def col_send(s, c2):
            col_copy(lax.rem(me_row + 1 + s, n_row), me_row, k).start()
            return c2

        lax.fori_loop(0, n_row - 1, col_send, 0)
        c_recv[k, me_row] = c_send[k]

        def row_done(s, c2):
            peer = lax.rem(me_col + 1 + s, n_col)
            scatter_copy(peer, me_col).wait_send()
            gather_copy(peer, me_col).wait_send()
            return c2

        lax.fori_loop(0, n_col - 1, row_done, 0)

        def col_wait(s, c2):
            col_copy(me_row, lax.rem(me_row + 1 + s, n_row), k).wait_recv()
            return c2

        lax.fori_loop(0, n_row - 1, col_wait, 0)
        u_ref[...] = u_ref[...] + (log2_b - log2_sum(c_recv[k])[0])
        b_ref[pl.ds(3 * dim, slab), :] = with_bias(bbase[...], u_ref[...], 3).astype(jnp.bfloat16)
        bt_ref[:, pl.ds(depth // 2, depth // 2)] = b_ref[pl.ds(depth // 2, depth // 2), :].T
        return carry

    lax.fori_loop(0, ITERS, iteration, 0)

    for q in range(n_col):
        potential = (t_ref[q] + nx_ref[q]) * (1.0 / kappa)
        for part in range(per):
            f_ref[pl.ds(q * per + part, 1), :] = potential[:, part * block : (part + 1) * block]
    potential = (u_ref[...] + ny_ref[...]) * (1.0 / kappa)
    for c in range(col_blocks):
        g_ref[pl.ds(c, 1), :] = potential[:, c * block : (c + 1) * block]

    def col_done(i, carry):
        peer = lax.rem(me_row + 1 + lax.rem(i, n_row - 1), n_row)
        col_copy(peer, me_row, i // (n_row - 1)).wait_send()
        return carry

    lax.fori_loop(0, ITERS * (n_row - 1), col_done, 0)


def body(n_row, n_col, row_points, col_points, block_lists):
    row_blocks, dim, block = row_points.shape
    col_blocks = col_points.shape[0]
    width = row_blocks // n_col * block
    cols = col_blocks * block
    f32, bf16 = jnp.float32, jnp.bfloat16
    pairs = row_blocks * col_blocks * block * block
    vmem = pl.BlockSpec(memory_space=pltpu.VMEM)
    return pl.pallas_call(
        functools.partial(kernel, n_row, n_col),
        out_shape=(
            jax.ShapeDtypeStruct((row_blocks, block), f32),
            jax.ShapeDtypeStruct((col_blocks, block), f32),
        ),
        in_specs=[vmem] * 3,
        out_specs=(vmem, vmem),
        scratch_shapes=[
            pltpu.VMEM((n_col, depth, width), bf16),
            pltpu.VMEM((n_col, width, depth), bf16),
            pltpu.VMEM((depth, cols), bf16),
            pltpu.VMEM((cols, depth), bf16),
            pltpu.VMEM((n_col, slab, width), f32),
            pltpu.VMEM((slab, cols), f32),
            pltpu.VMEM((n_col, 1, width), f32),
            pltpu.VMEM((1, cols), f32),
            pltpu.VMEM((n_col, 1, width), f32),
            pltpu.VMEM((1, cols), f32),
            pltpu.VMEM((n_col, 1, width), f32),
            pltpu.VMEM((n_col, 1, width), f32),
            pltpu.VMEM((n_col, 1, cols), f32),
            pltpu.VMEM((ITERS, 1, cols), f32),
            pltpu.VMEM((ITERS, n_row, 1, cols), f32),
            pltpu.VMEM((col_blocks, block, width), f32),
            pltpu.SemaphoreType.DMA((n_col,)),
            pltpu.SemaphoreType.DMA((n_col,)),
            pltpu.SemaphoreType.DMA((n_col,)),
            pltpu.SemaphoreType.DMA((n_col,)),
            pltpu.SemaphoreType.DMA((ITERS, n_row)),
            pltpu.SemaphoreType.DMA((ITERS, n_row)),
        ],
        compiler_params=pltpu.CompilerParams(
            collective_id=0, has_side_effects=True, vmem_limit_bytes=56 * 1024 * 1024
        ),
        cost_estimate=pl.CostEstimate(
            flops=2 * 2 * ITERS * pairs * depth,
            bytes_accessed=row_blocks * dim * block * 2,
            transcendentals=2 * ITERS * pairs,
        ),
    )(block_lists, row_points, col_points)


def solution(mesh):
    placed = (P("row", None, None), P("col", None, None), P("row", None))
    return jax.shard_map(
        functools.partial(body, mesh.shape["row"], mesh.shape["col"]),
        mesh=mesh,
        in_specs=placed,
        out_specs=(P("row", None), P("col", None)),
        check_vma=False,
    )
```

```python
import functools
import math

import jax
import jax.numpy as jnp
from jax import lax
from jax.experimental import pallas as pl
from jax.experimental.pallas import tpu as pltpu
from jax.sharding import PartitionSpec as P

ITERS = 4
eps_reg = 0.05
kappa = math.log2(math.e) / eps_reg
masked_score = -(2.0**40)
lift = 100.0
least, most = 2.0**-80, 2.0**126
depth = 256
slab = 16
MESH = pl.DeviceIdType.MESH


def split3(values):
    high = values.astype(jnp.bfloat16).astype(jnp.float32)
    rest = values - high
    mid = rest.astype(jnp.bfloat16).astype(jnp.float32)
    low = (rest - mid).astype(jnp.bfloat16).astype(jnp.float32)
    return high, mid, low


def with_bias(base, bias, first):
    rows = lax.broadcasted_iota(jnp.int32, base.shape, 0)
    high, mid, low = split3(bias)
    out = jnp.where(rows == first, high, base)
    out = jnp.where(rows == first + 1, mid, out)
    return jnp.where(rows == first + 2, low, out)


def log2_sum(parts):
    peak = jnp.max(parts, axis=0, keepdims=True)
    return peak + jnp.log2(jnp.sum(jnp.exp2(parts - peak), axis=0, keepdims=True))


def lifted_log2(total):
    inside = (total > least) & (total < most)
    return jnp.log2(jnp.where(inside, total, jnp.nan))


def kernel(
    exact, n_row, n_col, lists_ref, x_ref, y_ref, f_ref, g_ref, flag_ref,
    a_ref, at_ref, b_ref, bt_ref, abase, bbase, t_ref, u_ref, nx_ref, ny_ref,
    l_ref, rs_recv, lc_ref, c_send, c_recv, s_ref, sums_ref, flag_recv,
    rs_ssem, rs_rsem, ag_ssem, ag_rsem, c_ssem, c_rsem, flag_ssem, flag_rsem,
):
    me_row = lax.axis_index("row")
    me_col = lax.axis_index("col")
    row_blocks, dim, block = x_ref.shape
    col_blocks = y_ref.shape[0]
    per = row_blocks // n_col
    width = per * block
    cols = col_blocks * block
    log2_a = -math.log2(n_row * row_blocks * block)
    log2_b = -math.log2(n_col * cols)
    alpha = 2.0 * kappa / dim
    beta = kappa / dim
    raise_by = 0.0 if exact else lift

    barrier = pltpu.get_barrier_semaphore()
    for step in range(1, n_col):
        pl.semaphore_signal(
            barrier, inc=1, device_id={"col": lax.rem(me_col + step, n_col)}, device_id_type=MESH
        )
    for step in range(1, n_row):
        pl.semaphore_signal(
            barrier, inc=1, device_id={"row": lax.rem(me_row + step, n_row)}, device_id_type=MESH
        )

    slab_rows = lax.broadcasted_iota(jnp.int32, (slab, block), 0)
    zeros = jnp.zeros((depth - 3 * dim - slab, block), jnp.bfloat16)

    for c in range(col_blocks):
        lanes = pl.ds(c * block, block)
        y = y_ref[c]
        for part in range(3):
            b_ref[pl.ds(part * dim, dim), lanes] = y
        y32 = y.astype(jnp.float32)
        norm = jnp.sum(y32 * y32, axis=0, keepdims=True) * beta
        ny_ref[:, lanes] = norm
        u_ref[:, lanes] = -norm
        base = jnp.where((slab_rows < 3) | (slab_rows == 6 + c), 1.0, 0.0)
        bbase[:, lanes] = base
        b_ref[pl.ds(3 * dim, slab), lanes] = with_bias(base, -norm, 3).astype(jnp.bfloat16)
        b_ref[pl.ds(3 * dim + slab, depth - 3 * dim - slab), lanes] = zeros
        bt_ref[pl.ds(c * block, block), :] = b_ref[:, lanes].T

    def prepare(q, carry):
        for part in range(per):
            r = q * per + part
            lanes = pl.ds(part * block, block)
            x = x_ref[r].astype(jnp.float32)
            norm = jnp.sum(x * x, axis=0, keepdims=True) * beta
            nx_ref[q, :, lanes] = norm
            t_ref[q, :, lanes] = -norm
            for i, piece in enumerate(split3(x * alpha)):
                a_ref[q, pl.ds(i * dim, dim), lanes] = piece.astype(jnp.bfloat16)
            listed = lists_ref[pl.ds(r, 1), :]
            base = jnp.where((slab_rows >= 3) & (slab_rows < 6), 1.0, 0.0)
            for c in range(col_blocks):
                hit = jnp.where(listed == me_col * col_blocks + c, 1.0, 0.0)
                hit = jnp.max(hit, axis=1, keepdims=True)
                fill = jnp.broadcast_to(jnp.where(hit > 0.0, 0.0, masked_score), (slab, block))
                base = jnp.where(slab_rows == 6 + c, fill, base)
            abase[q, :, lanes] = base
            a_ref[q, pl.ds(3 * dim, slab), lanes] = with_bias(base, raise_by - norm, 0).astype(jnp.bfloat16)
            a_ref[q, pl.ds(3 * dim + slab, depth - 3 * dim - slab), lanes] = zeros
            at_ref[q, pl.ds(part * block, block), :] = a_ref[q, :, lanes].T
        return carry

    lax.fori_loop(0, n_col, prepare, 0)
    pl.semaphore_wait(barrier, n_col - 1 + n_row - 1)

    def row_part(q):
        points = a_ref[q]
        if not exact:
            total = jnp.zeros((8, width), jnp.float32)
            for c in range(col_blocks):
                scores = jnp.dot(
                    bt_ref[pl.ds(c * block, block), :], points, preferred_element_type=jnp.float32
                )
                total += jnp.sum(jnp.exp2(scores).reshape(block // 8, 8, width), axis=0)
            return jnp.sum(total, axis=0, keepdims=True)
        peak = None
        for c in range(col_blocks):
            scores = jnp.dot(
                bt_ref[pl.ds(c * block, block), :], points, preferred_element_type=jnp.float32
            )
            s_ref[c] = scores
            top = jnp.max(scores.reshape(block // 8, 8, width), axis=0)
            peak = top if peak is None else jnp.maximum(peak, top)
        peak = jnp.max(peak, axis=0, keepdims=True)
        total = jnp.zeros((8, width), jnp.float32)
        for c in range(col_blocks):
            total += jnp.sum(jnp.exp2(s_ref[c] - peak).reshape(block // 8, 8, width), axis=0)
        return peak + jnp.log2(jnp.sum(total, axis=0, keepdims=True))

    def scatter_copy(peer, slot):
        return pltpu.make_async_remote_copy(
            src_ref=l_ref.at[peer], dst_ref=rs_recv.at[slot],
            send_sem=rs_ssem.at[peer], recv_sem=rs_rsem.at[slot],
            device_id={"col": peer}, device_id_type=MESH,
        )

    def gather_copy(peer, slot):
        return pltpu.make_async_remote_copy(
            src_ref=t_ref.at[slot], dst_ref=t_ref.at[slot],
            send_sem=ag_ssem.at[peer], recv_sem=ag_rsem.at[slot],
            device_id={"col": peer}, device_id_type=MESH,
        )

    def col_copy(peer, slot, k):
        return pltpu.make_async_remote_copy(
            src_ref=c_send.at[k], dst_ref=c_recv.at[k, slot],
            send_sem=c_ssem.at[k, peer], recv_sem=c_rsem.at[k, slot],
            device_id={"row": peer}, device_id_type=MESH,
        )

    def combined(parts):
        if exact:
            return log2_sum(parts)[0]
        return lifted_log2(jnp.sum(parts, axis=0))

    def iteration(k, carry):
        def row_step(s, c2):
            q = lax.rem(me_col + 1 + s, n_col)
            l_ref[q] = row_part(q)

            @pl.when(s < n_col - 1)
            def _():
                scatter_copy(q, me_col).start()

            return c2

        lax.fori_loop(0, n_col, row_step, 0)
        rs_recv[me_col] = l_ref[me_col]

        def row_wait(s, c2):
            scatter_copy(me_col, lax.rem(me_col + 1 + s, n_col)).wait_recv()
            return c2

        lax.fori_loop(0, n_col - 1, row_wait, 0)
        t_ref[me_col] = t_ref[me_col] + ((log2_a + raise_by) - combined(rs_recv[...]))

        def row_send(s, c2):
            gather_copy(lax.rem(me_col + 1 + s, n_col), me_col).start()
            return c2

        lax.fori_loop(0, n_col - 1, row_send, 0)

        def col_step(s, c2):
            q = lax.rem(me_col + s, n_col)

            @pl.when(s > 0)
            def _():
                gather_copy(me_col, q).wait_recv()

            a_ref[q, pl.ds(3 * dim, slab), :] = with_bias(abase[q], t_ref[q] + raise_by, 0).astype(
                jnp.bfloat16
            )
            at_ref[q, :, pl.ds(depth // 2, depth // 2)] = a_ref[
                q, pl.ds(depth // 2, depth // 2), :
            ].T
            points = at_ref[q]
            for c in range(col_blocks):
                lanes = pl.ds(c * block, block)
                scores = jnp.dot(points, b_ref[:, lanes], preferred_element_type=jnp.float32)
                if exact:
                    peak = jnp.max(scores, axis=0, keepdims=True)
                    total = jnp.sum(jnp.exp2(scores - peak), axis=0, keepdims=True)
                    lc_ref[q, :, lanes] = peak + jnp.log2(total)
                else:
                    sums_ref[:, lanes] += jnp.sum(
                        jnp.exp2(scores).reshape(width // 8, 8, block), axis=0
                    )
            return c2

        sums_ref[...] = jnp.zeros((8, cols), jnp.float32)
        lax.fori_loop(0, n_col, col_step, 0)
        if exact:
            c_send[k] = log2_sum(lc_ref[...])[0]
        else:
            c_send[k] = jnp.sum(sums_ref[...], axis=0, keepdims=True)

        def col_send(s, c2):
            col_copy(lax.rem(me_row + 1 + s, n_row), me_row, k).start()
            return c2

        lax.fori_loop(0, n_row - 1, col_send, 0)
        c_recv[k, me_row] = c_send[k]

        def row_done(s, c2):
            peer = lax.rem(me_col + 1 + s, n_col)
            scatter_copy(peer, me_col).wait_send()
            gather_copy(peer, me_col).wait_send()
            return c2

        lax.fori_loop(0, n_col - 1, row_done, 0)

        def col_wait(s, c2):
            col_copy(me_row, lax.rem(me_row + 1 + s, n_row), k).wait_recv()
            return c2

        lax.fori_loop(0, n_row - 1, col_wait, 0)
        u_ref[...] = u_ref[...] + ((log2_b + raise_by) - combined(c_recv[k]))
        b_ref[pl.ds(3 * dim, slab), :] = with_bias(bbase[...], u_ref[...], 3).astype(jnp.bfloat16)
        bt_ref[:, pl.ds(depth // 2, depth // 2)] = b_ref[pl.ds(depth // 2, depth // 2), :].T
        return carry

    lax.fori_loop(0, ITERS, iteration, 0)

    def flag_copy(peer, slot):
        return pltpu.make_async_remote_copy(
            src_ref=flag_recv.at[slot], dst_ref=flag_recv.at[slot],
            send_sem=flag_ssem.at[peer], recv_sem=flag_rsem.at[slot],
            device_id={"col": peer}, device_id_type=MESH,
        )

    def flag_send(s, carry):
        flag_copy(lax.rem(me_col + 1 + s, n_col), me_col).start()
        return carry

    def flag_wait(s, carry):
        peer = lax.rem(me_col + 1 + s, n_col)
        flag_copy(me_col, peer).wait_recv()
        flag_copy(peer, me_col).wait_send()
        return carry

    if not exact:
        flag_recv[me_col] = sum(u_ref[:, i * 128 : (i + 1) * 128] for i in range(cols // 128))
        lax.fori_loop(0, n_col - 1, flag_send, 0)

    for q in range(n_col):
        potential = (t_ref[q] + nx_ref[q]) * (1.0 / kappa)
        for part in range(per):
            f_ref[pl.ds(q * per + part, 1), :] = potential[:, part * block : (part + 1) * block]
    potential = (u_ref[...] + ny_ref[...]) * (1.0 / kappa)
    for c in range(col_blocks):
        g_ref[pl.ds(c, 1), :] = potential[:, c * block : (c + 1) * block]

    def col_done(i, carry):
        peer = lax.rem(me_row + 1 + lax.rem(i, n_row - 1), n_row)
        col_copy(peer, me_row, i // (n_row - 1)).wait_send()
        return carry

    lax.fori_loop(0, ITERS * (n_row - 1), col_done, 0)
    if exact:
        flag_ref[...] = jnp.zeros_like(flag_ref)
    else:
        lax.fori_loop(0, n_col - 1, flag_wait, 0)
        seen = jnp.sum(jnp.sum(flag_recv[...], axis=0), axis=1, keepdims=True)
        flag_ref[...] = jnp.broadcast_to(jnp.where(seen == seen, 0, 1), flag_ref.shape)


def run(exact, n_row, n_col, row_points, col_points, block_lists):
    row_blocks, dim, block = row_points.shape
    col_blocks = col_points.shape[0]
    width = row_blocks // n_col * block
    cols = col_blocks * block
    f32, bf16 = jnp.float32, jnp.bfloat16
    pairs = row_blocks * col_blocks * block * block
    vmem = pl.BlockSpec(memory_space=pltpu.VMEM)
    return pl.pallas_call(
        functools.partial(kernel, exact, n_row, n_col),
        out_shape=(
            jax.ShapeDtypeStruct((row_blocks, block), f32),
            jax.ShapeDtypeStruct((col_blocks, block), f32),
            jax.ShapeDtypeStruct((1, 128), jnp.int32),
        ),
        in_specs=[vmem] * 3,
        out_specs=(vmem, vmem, vmem),
        scratch_shapes=[
            pltpu.VMEM((n_col, depth, width), bf16),
            pltpu.VMEM((n_col, width, depth), bf16),
            pltpu.VMEM((depth, cols), bf16),
            pltpu.VMEM((cols, depth), bf16),
            pltpu.VMEM((n_col, slab, width), f32),
            pltpu.VMEM((slab, cols), f32),
            pltpu.VMEM((n_col, 1, width), f32),
            pltpu.VMEM((1, cols), f32),
            pltpu.VMEM((n_col, 1, width), f32),
            pltpu.VMEM((1, cols), f32),
            pltpu.VMEM((n_col, 1, width), f32),
            pltpu.VMEM((n_col, 1, width), f32),
            pltpu.VMEM((n_col, 1, cols), f32),
            pltpu.VMEM((ITERS, 1, cols), f32),
            pltpu.VMEM((ITERS, n_row, 1, cols), f32),
            pltpu.VMEM((col_blocks, block, width) if exact else (1, 8, 128), f32),
            pltpu.VMEM((8, cols), f32),
            pltpu.VMEM((n_col, 1, 128), f32),
            pltpu.SemaphoreType.DMA((n_col,)),
            pltpu.SemaphoreType.DMA((n_col,)),
            pltpu.SemaphoreType.DMA((n_col,)),
            pltpu.SemaphoreType.DMA((n_col,)),
            pltpu.SemaphoreType.DMA((ITERS, n_row)),
            pltpu.SemaphoreType.DMA((ITERS, n_row)),
            pltpu.SemaphoreType.DMA((n_col,)),
            pltpu.SemaphoreType.DMA((n_col,)),
        ],
        compiler_params=pltpu.CompilerParams(
            collective_id=int(exact), has_side_effects=True, vmem_limit_bytes=56 * 1024 * 1024
        ),
        cost_estimate=pl.CostEstimate(
            flops=2 * 2 * ITERS * pairs * depth,
            bytes_accessed=row_blocks * dim * block * 2,
            transcendentals=2 * ITERS * pairs,
        ),
    )(block_lists, row_points, col_points)


def body(n_row, n_col, *arguments):
    row_potential, col_potential, flag = run(False, n_row, n_col, *arguments)
    return lax.cond(
        flag[0, 0] > 0,
        lambda *operands: run(True, n_row, n_col, *operands[2:])[:2],
        lambda *operands: operands[:2],
        row_potential,
        col_potential,
        *arguments,
    )


def solution(mesh):
    placed = (P("row", None, None), P("col", None, None), P("row", None))
    return jax.shard_map(
        functools.partial(body, mesh.shape["row"], mesh.shape["col"]),
        mesh=mesh,
        in_specs=placed,
        out_specs=(P("row", None), P("col", None)),
        check_vma=False,
    )
```

```python
import functools
import math

import jax
import jax.numpy as jnp
from jax import lax
from jax.experimental import pallas as pl
from jax.experimental.pallas import tpu as pltpu
from jax.sharding import PartitionSpec as P

ITERS = 4
eps_reg = 0.05
kappa = math.log2(math.e) / eps_reg
masked_score = -(2.0**40)
lift = 100.0
least, most = 2.0**-80, 2.0**126
depth = 256
group = 4
slab = 16
MESH = pl.DeviceIdType.MESH


def split3(values):
    high = values.astype(jnp.bfloat16).astype(jnp.float32)
    rest = values - high
    mid = rest.astype(jnp.bfloat16).astype(jnp.float32)
    low = (rest - mid).astype(jnp.bfloat16).astype(jnp.float32)
    return high, mid, low


def with_bias(base, bias, first):
    rows = lax.broadcasted_iota(jnp.int32, base.shape, 0)
    high, mid, low = split3(bias)
    out = jnp.where(rows == first, high, base)
    out = jnp.where(rows == first + 1, mid, out)
    return jnp.where(rows == first + 2, low, out)


def log2_sum(parts):
    peak = jnp.max(parts, axis=0, keepdims=True)
    return peak + jnp.log2(jnp.sum(jnp.exp2(parts - peak), axis=0, keepdims=True))


def lifted_log2(total):
    inside = (total > least) & (total < most)
    return jnp.log2(jnp.where(inside, total, jnp.nan))


def kernel(
    exact, n_row, n_col, lists_ref, x_ref, y_ref, f_ref, g_ref, flag_ref,
    a_ref, at_ref, b_ref, bt_ref, abase, bbase, t_ref, u_ref, nx_ref, ny_ref,
    l_ref, rs_recv, lc_ref, c_send, c_recv, s_ref, sums_ref, flag_recv,
    rs_ssem, rs_rsem, ag_ssem, ag_rsem, c_ssem, c_rsem, flag_ssem, flag_rsem,
):
    me_row = lax.axis_index("row")
    me_col = lax.axis_index("col")
    row_blocks, dim, block = x_ref.shape
    col_blocks = y_ref.shape[0]
    per = row_blocks // n_col
    width = per * block
    cols = col_blocks * block
    log2_a = -math.log2(n_row * row_blocks * block)
    log2_b = -math.log2(n_col * cols)
    alpha = 2.0 * kappa / dim
    beta = kappa / dim
    raise_by = 0.0 if exact else lift

    barrier = pltpu.get_barrier_semaphore()
    for step in range(1, n_col):
        pl.semaphore_signal(
            barrier, inc=1, device_id={"col": lax.rem(me_col + step, n_col)}, device_id_type=MESH
        )
    for step in range(1, n_row):
        pl.semaphore_signal(
            barrier, inc=1, device_id={"row": lax.rem(me_row + step, n_row)}, device_id_type=MESH
        )

    slab_rows = lax.broadcasted_iota(jnp.int32, (slab, block), 0)
    zeros = jnp.zeros((depth - 3 * dim - slab, block), jnp.bfloat16)

    for c in range(col_blocks):
        lanes = pl.ds(c * block, block)
        y = y_ref[c]
        for part in range(3):
            b_ref[pl.ds(part * dim, dim), lanes] = y
        y32 = y.astype(jnp.float32)
        norm = jnp.sum(y32 * y32, axis=0, keepdims=True) * beta
        ny_ref[:, lanes] = norm
        u_ref[:, lanes] = -norm
        base = jnp.where((slab_rows < 3) | (slab_rows == 6 + c), 1.0, 0.0)
        bbase[:, lanes] = base
        b_ref[pl.ds(3 * dim, slab), lanes] = with_bias(base, -norm, 3).astype(jnp.bfloat16)
        b_ref[pl.ds(3 * dim + slab, depth - 3 * dim - slab), lanes] = zeros
        bt_ref[pl.ds(c * block, block), :] = b_ref[:, lanes].T

    def prepare(q, carry):
        for part in range(per):
            r = q * per + part
            lanes = pl.ds(part * block, block)
            x = x_ref[r].astype(jnp.float32)
            norm = jnp.sum(x * x, axis=0, keepdims=True) * beta
            nx_ref[q, :, lanes] = norm
            t_ref[q, :, lanes] = -norm
            for i, piece in enumerate(split3(x * alpha)):
                a_ref[q, pl.ds(i * dim, dim), lanes] = piece.astype(jnp.bfloat16)
            listed = lists_ref[pl.ds(r, 1), :]
            base = jnp.where((slab_rows >= 3) & (slab_rows < 6), 1.0, 0.0)
            for c in range(col_blocks):
                hit = jnp.where(listed == me_col * col_blocks + c, 1.0, 0.0)
                hit = jnp.max(hit, axis=1, keepdims=True)
                fill = jnp.broadcast_to(jnp.where(hit > 0.0, 0.0, masked_score), (slab, block))
                base = jnp.where(slab_rows == 6 + c, fill, base)
            abase[q, :, lanes] = base
            a_ref[q, pl.ds(3 * dim, slab), lanes] = with_bias(base, raise_by - norm, 0).astype(jnp.bfloat16)
            a_ref[q, pl.ds(3 * dim + slab, depth - 3 * dim - slab), lanes] = zeros
            at_ref[q, pl.ds(part * block, block), :] = a_ref[q, :, lanes].T
        return carry

    lax.fori_loop(0, n_col, prepare, 0)
    pl.semaphore_wait(barrier, n_col - 1 + n_row - 1)

    def row_part(q):
        points = a_ref[q]
        if not exact:
            total = jnp.zeros((8, width), jnp.float32)
            for c in range(col_blocks):
                scores = jnp.dot(
                    bt_ref[pl.ds(c * block, block), :], points, preferred_element_type=jnp.float32
                )
                total += jnp.sum(jnp.exp2(scores).reshape(block // 8, 8, width), axis=0)
            return jnp.sum(total, axis=0, keepdims=True)
        peak = None
        for c in range(col_blocks):
            scores = jnp.dot(
                bt_ref[pl.ds(c * block, block), :], points, preferred_element_type=jnp.float32
            )
            s_ref[c] = scores
            top = jnp.max(scores.reshape(block // 8, 8, width), axis=0)
            peak = top if peak is None else jnp.maximum(peak, top)
        peak = jnp.max(peak, axis=0, keepdims=True)
        total = jnp.zeros((8, width), jnp.float32)
        for c in range(col_blocks):
            total += jnp.sum(jnp.exp2(s_ref[c] - peak).reshape(block // 8, 8, width), axis=0)
        return peak + jnp.log2(jnp.sum(total, axis=0, keepdims=True))

    def scatter_copy(peer, slot):
        return pltpu.make_async_remote_copy(
            src_ref=l_ref.at[peer], dst_ref=rs_recv.at[slot],
            send_sem=rs_ssem.at[peer], recv_sem=rs_rsem.at[slot],
            device_id={"col": peer}, device_id_type=MESH,
        )

    def gather_copy(peer, slot):
        return pltpu.make_async_remote_copy(
            src_ref=t_ref.at[slot], dst_ref=t_ref.at[slot],
            send_sem=ag_ssem.at[peer], recv_sem=ag_rsem.at[slot],
            device_id={"col": peer}, device_id_type=MESH,
        )

    def col_copy(peer, slot, k):
        return pltpu.make_async_remote_copy(
            src_ref=c_send.at[k], dst_ref=c_recv.at[k, slot],
            send_sem=c_ssem.at[k, peer], recv_sem=c_rsem.at[k, slot],
            device_id={"row": peer}, device_id_type=MESH,
        )

    def combined(parts):
        if exact:
            return log2_sum(parts)[0]
        return lifted_log2(jnp.sum(parts, axis=0))

    def iteration(k, carry):
        def row_step(s, c2):
            q = lax.rem(me_col + 1 + s, n_col)
            l_ref[q] = row_part(q)

            @pl.when(s < n_col - 1)
            def _():
                scatter_copy(q, me_col).start()

            return c2

        lax.fori_loop(0, n_col, row_step, 0)
        rs_recv[me_col] = l_ref[me_col]

        def row_wait(s, c2):
            scatter_copy(me_col, lax.rem(me_col + 1 + s, n_col)).wait_recv()
            return c2

        lax.fori_loop(0, n_col - 1, row_wait, 0)
        t_ref[me_col] = t_ref[me_col] + ((log2_a + raise_by) - combined(rs_recv[...]))

        def row_send(s, c2):
            gather_copy(lax.rem(me_col + 1 + s, n_col), me_col).start()
            return c2

        lax.fori_loop(0, n_col - 1, row_send, 0)

        def col_step(s, c2):
            q = lax.rem(me_col + s, n_col)

            @pl.when(s > 0)
            def _():
                gather_copy(me_col, q).wait_recv()

            a_ref[q, pl.ds(3 * dim, slab), :] = with_bias(abase[q], t_ref[q] + raise_by, 0).astype(
                jnp.bfloat16
            )
            at_ref[q, :, pl.ds(depth // 2, depth // 2)] = a_ref[
                q, pl.ds(depth // 2, depth // 2), :
            ].T
            points = at_ref[q]
            for c in range(col_blocks):
                lanes = pl.ds(c * block, block)
                scores = jnp.dot(points, b_ref[:, lanes], preferred_element_type=jnp.float32)
                if exact:
                    peak = jnp.max(scores, axis=0, keepdims=True)
                    total = jnp.sum(jnp.exp2(scores - peak), axis=0, keepdims=True)
                    lc_ref[q, :, lanes] = peak + jnp.log2(total)
                else:
                    sums_ref[:, lanes] += jnp.sum(
                        jnp.exp2(scores).reshape(width // 8, 8, block), axis=0
                    )
            return c2

        sums_ref[...] = jnp.zeros((8, cols), jnp.float32)
        lax.fori_loop(0, n_col, col_step, 0)
        if exact:
            c_send[k] = log2_sum(lc_ref[...])[0]
        else:
            c_send[k] = jnp.sum(sums_ref[...], axis=0, keepdims=True)

        def col_send(s, c2):
            col_copy(lax.rem(me_row + 1 + s, n_row), me_row, k).start()
            return c2

        lax.fori_loop(0, n_row - 1, col_send, 0)
        c_recv[k, me_row] = c_send[k]

        def row_done(s, c2):
            peer = lax.rem(me_col + 1 + s, n_col)
            scatter_copy(peer, me_col).wait_send()
            gather_copy(peer, me_col).wait_send()
            return c2

        lax.fori_loop(0, n_col - 1, row_done, 0)

        def col_wait(s, c2):
            col_copy(me_row, lax.rem(me_row + 1 + s, n_row), k).wait_recv()
            return c2

        lax.fori_loop(0, n_row - 1, col_wait, 0)
        u_ref[...] = u_ref[...] + ((log2_b + raise_by) - combined(c_recv[k]))
        b_ref[pl.ds(3 * dim, slab), :] = with_bias(bbase[...], u_ref[...], 3).astype(jnp.bfloat16)
        bt_ref[:, pl.ds(depth // 2, depth // 2)] = b_ref[pl.ds(depth // 2, depth // 2), :].T
        return carry

    lax.fori_loop(0, ITERS, iteration, 0)

    def flag_copy(peer, slot):
        return pltpu.make_async_remote_copy(
            src_ref=flag_recv.at[slot], dst_ref=flag_recv.at[slot],
            send_sem=flag_ssem.at[peer], recv_sem=flag_rsem.at[slot],
            device_id={"col": peer}, device_id_type=MESH,
        )

    def flag_send(s, carry):
        flag_copy(lax.rem(me_col + 1 + s, n_col), me_col).start()
        return carry

    def flag_wait(s, carry):
        peer = lax.rem(me_col + 1 + s, n_col)
        flag_copy(me_col, peer).wait_recv()
        flag_copy(peer, me_col).wait_send()
        return carry

    if not exact:
        flag_recv[me_col] = sum(u_ref[:, i * 128 : (i + 1) * 128] for i in range(cols // 128))
        lax.fori_loop(0, n_col - 1, flag_send, 0)

    for q in range(n_col):
        potential = (t_ref[q] + nx_ref[q]) * (1.0 / kappa)
        for part in range(per):
            f_ref[pl.ds(q * per + part, 1), :] = potential[:, part * block : (part + 1) * block]
    potential = (u_ref[...] + ny_ref[...]) * (1.0 / kappa)
    for c in range(col_blocks):
        g_ref[pl.ds(c, 1), :] = potential[:, c * block : (c + 1) * block]

    def col_done(i, carry):
        peer = lax.rem(me_row + 1 + lax.rem(i, n_row - 1), n_row)
        col_copy(peer, me_row, i // (n_row - 1)).wait_send()
        return carry

    lax.fori_loop(0, ITERS * (n_row - 1), col_done, 0)
    if exact:
        flag_ref[...] = jnp.zeros_like(flag_ref)
    else:
        lax.fori_loop(0, n_col - 1, flag_wait, 0)
        seen = jnp.sum(jnp.sum(flag_recv[...], axis=0), axis=1, keepdims=True)
        flag_ref[...] = jnp.broadcast_to(jnp.where(seen == seen, 0, 1), flag_ref.shape)


def run(exact, n_row, n_col, row_points, col_points, block_lists):
    row_blocks, dim, block = row_points.shape
    col_blocks = col_points.shape[0]
    width = row_blocks // n_col * block
    cols = col_blocks * block
    f32, bf16 = jnp.float32, jnp.bfloat16
    pairs = row_blocks * col_blocks * block * block
    vmem = pl.BlockSpec(memory_space=pltpu.VMEM)
    return pl.pallas_call(
        functools.partial(kernel, exact, n_row, n_col),
        out_shape=(
            jax.ShapeDtypeStruct((row_blocks, block), f32),
            jax.ShapeDtypeStruct((col_blocks, block), f32),
            jax.ShapeDtypeStruct((1, 128), jnp.int32),
        ),
        in_specs=[vmem] * 3,
        out_specs=(vmem, vmem, vmem),
        scratch_shapes=[
            pltpu.VMEM((n_col, depth, width), bf16),
            pltpu.VMEM((n_col, width, depth), bf16),
            pltpu.VMEM((depth, cols), bf16),
            pltpu.VMEM((cols, depth), bf16),
            pltpu.VMEM((n_col, slab, width), f32),
            pltpu.VMEM((slab, cols), f32),
            pltpu.VMEM((n_col, 1, width), f32),
            pltpu.VMEM((1, cols), f32),
            pltpu.VMEM((n_col, 1, width), f32),
            pltpu.VMEM((1, cols), f32),
            pltpu.VMEM((n_col, 1, width), f32),
            pltpu.VMEM((n_col, 1, width), f32),
            pltpu.VMEM((n_col, 1, cols), f32),
            pltpu.VMEM((ITERS, 1, cols), f32),
            pltpu.VMEM((ITERS, n_row, 1, cols), f32),
            pltpu.VMEM((col_blocks, block, width) if exact else (1, 8, 128), f32),
            pltpu.VMEM((8, cols), f32),
            pltpu.VMEM((n_col, 1, 128), f32),
            pltpu.SemaphoreType.DMA((n_col,)),
            pltpu.SemaphoreType.DMA((n_col,)),
            pltpu.SemaphoreType.DMA((n_col,)),
            pltpu.SemaphoreType.DMA((n_col,)),
            pltpu.SemaphoreType.DMA((ITERS, n_row)),
            pltpu.SemaphoreType.DMA((ITERS, n_row)),
            pltpu.SemaphoreType.DMA((n_col,)),
            pltpu.SemaphoreType.DMA((n_col,)),
        ],
        compiler_params=pltpu.CompilerParams(
            collective_id=int(exact), has_side_effects=True, vmem_limit_bytes=56 * 1024 * 1024
        ),
        cost_estimate=pl.CostEstimate(
            flops=2 * 2 * ITERS * pairs * depth,
            bytes_accessed=row_blocks * dim * block * 2,
            transcendentals=2 * ITERS * pairs,
        ),
    )(block_lists, row_points, col_points)


def fast_kernel(
    n_row, n_col, lists_ref, x_ref, y_ref, f_ref, g_ref, flag_ref,
    a_ref, at_ref, b_ref, bt_ref, abase, bbase, t_ref, u_ref, nx_ref, ny_ref,
    l_ref, rs_recv, c_send, c_recv, sums_ref, flag_recv,
    rs_ssem, rs_rsem, ag_ssem, ag_rsem, c_ssem, c_rsem, flag_ssem, flag_rsem,
):
    me_row = lax.axis_index("row")
    me_col = lax.axis_index("col")
    row_blocks, dim, block = x_ref.shape
    col_blocks = y_ref.shape[0]
    per = row_blocks // n_col
    part_width = per * block // 2
    cols = col_blocks * block
    half = cols // 2
    log2_a = -math.log2(n_row * row_blocks * block)
    log2_b = -math.log2(n_col * cols)
    alpha = 2.0 * kappa / dim
    beta = kappa / dim
    bias_rows = pl.ds(3 * dim, slab)
    spare_rows = pl.ds(3 * dim + slab, depth - 3 * dim - slab)
    changing = pl.ds(depth // 2, depth // 2)

    barrier = pltpu.get_barrier_semaphore()
    for step in range(1, n_col):
        pl.semaphore_signal(
            barrier, inc=1, device_id={"col": lax.rem(me_col + step, n_col)}, device_id_type=MESH
        )
    for step in range(1, n_row):
        pl.semaphore_signal(
            barrier, inc=1, device_id={"row": lax.rem(me_row + step, n_row)}, device_id_type=MESH
        )

    slab_rows = lax.broadcasted_iota(jnp.int32, (slab, block), 0)
    zeros = jnp.zeros((depth - 3 * dim - slab, block), jnp.bfloat16)

    for c in range(col_blocks):
        lanes = pl.ds(c * block, block)
        y = y_ref[c]
        for part in range(3):
            b_ref[pl.ds(part * dim, dim), lanes] = y
        y32 = y.astype(jnp.float32)
        norm = jnp.sum(y32 * y32, axis=0, keepdims=True) * beta
        ny_ref[:, lanes] = norm
        u_ref[:, lanes] = -norm
        base = jnp.where((slab_rows < 3) | (slab_rows == 6 + c), 1.0, 0.0)
        bbase[:, lanes] = base
        b_ref[bias_rows, lanes] = with_bias(base, -norm, 3).astype(jnp.bfloat16)
        b_ref[spare_rows, lanes] = zeros
        bt_ref[pl.ds(c * block, block), :] = b_ref[:, lanes].T

    def prepare(q, carry):
        for i in range(per):
            r = q * per + i
            lanes = pl.ds(i * block, block)
            x = x_ref[r].astype(jnp.float32)
            norm = jnp.sum(x * x, axis=0, keepdims=True) * beta
            part, inner = divmod(i * block, part_width)
            nx_ref[part, q, :, pl.ds(inner, block)] = norm
            t_ref[part, q, :, pl.ds(inner, block)] = -norm
            for j, piece in enumerate(split3(x * alpha)):
                a_ref[q, pl.ds(j * dim, dim), lanes] = piece.astype(jnp.bfloat16)
            listed = lists_ref[pl.ds(r, 1), :]
            base = jnp.where((slab_rows >= 3) & (slab_rows < 6), 1.0, 0.0)
            for c in range(col_blocks):
                hit = jnp.where(listed == me_col * col_blocks + c, 1.0, 0.0)
                hit = jnp.max(hit, axis=1, keepdims=True)
                fill = jnp.broadcast_to(jnp.where(hit > 0.0, 0.0, masked_score), (slab, block))
                base = jnp.where(slab_rows == 6 + c, fill, base)
            abase[q, :, lanes] = base
            a_ref[q, bias_rows, lanes] = with_bias(base, lift - norm, 0).astype(jnp.bfloat16)
            a_ref[q, spare_rows, lanes] = zeros
            at_ref[q, pl.ds(i * block, block), :] = a_ref[q, :, lanes].T
        return carry

    lax.fori_loop(0, n_col, prepare, 0)
    pl.semaphore_wait(barrier, n_col - 1 + n_row - 1)

    def scatter_copy(p, peer, slot):
        return pltpu.make_async_remote_copy(
            src_ref=l_ref.at[p, peer], dst_ref=rs_recv.at[p, slot],
            send_sem=rs_ssem.at[p, peer], recv_sem=rs_rsem.at[p, slot],
            device_id={"col": peer}, device_id_type=MESH,
        )

    def gather_copy(p, peer, slot):
        return pltpu.make_async_remote_copy(
            src_ref=t_ref.at[p, slot], dst_ref=t_ref.at[p, slot],
            send_sem=ag_ssem.at[p, peer], recv_sem=ag_rsem.at[p, slot],
            device_id={"col": peer}, device_id_type=MESH,
        )

    def col_copy(k, h, peer, slot):
        return pltpu.make_async_remote_copy(
            src_ref=c_send.at[k, h], dst_ref=c_recv.at[k, h, slot],
            send_sem=c_ssem.at[k, h, peer], recv_sem=c_rsem.at[k, h, slot],
            device_id={"row": peer}, device_id_type=MESH,
        )

    def flag_copy(peer, slot):
        return pltpu.make_async_remote_copy(
            src_ref=flag_recv.at[slot], dst_ref=flag_recv.at[slot],
            send_sem=flag_ssem.at[peer], recv_sem=flag_rsem.at[slot],
            device_id={"col": peer}, device_id_type=MESH,
        )

    col_peers = [lax.rem(me_col + step, n_col) for step in range(1, n_col)]
    row_peers = [lax.rem(me_row + step, n_row) for step in range(1, n_row)]

    def row_quarter(h, p):
        def step(s, carry):
            slices = [lax.rem(me_col + 1 + s * group + i, n_col) for i in range(group)]
            totals = []
            for q in slices:
                scores = jnp.dot(
                    bt_ref[pl.ds(h * half, half), :],
                    a_ref[q, :, pl.ds(p * part_width, part_width)],
                    preferred_element_type=jnp.float32,
                )
                total = jnp.sum(jnp.exp2(scores).reshape(half // 8, 8, part_width), axis=0)
                totals.append(jnp.sum(total, axis=0, keepdims=True))
            for i, q in enumerate(slices):
                l_ref[p, q] = totals[i] if h == 0 else l_ref[p, q] + totals[i]
            if h == 1:
                for q in slices[:-1]:
                    scatter_copy(p, q, me_col).start()

                @pl.when(s < n_col // group - 1)
                def _():
                    scatter_copy(p, slices[-1], me_col).start()

            return carry

        lax.fori_loop(0, n_col // group, step, 0)

    def col_quarter(h, p):
        lanes = pl.ds(h * half, half)
        points = pl.ds(p * part_width, part_width)

        def step(s, total):
            slices = [lax.rem(me_col + s * group + i, n_col) for i in range(group)]
            if h == 0:
                for q in slices:
                    a_ref[q, bias_rows, points] = with_bias(
                        abase[q, :, points], t_ref[p, q] + lift, 0
                    ).astype(jnp.bfloat16)
                    at_ref[q, points, changing] = a_ref[q, changing, points].T
            for q in slices:
                scores = jnp.dot(
                    at_ref[q, points, :], b_ref[:, lanes], preferred_element_type=jnp.float32
                )
                total += jnp.sum(jnp.exp2(scores).reshape(part_width // 8, 8, half), axis=0)
            return total

        start = jnp.zeros((8, half), jnp.float32) if p == 0 else sums_ref[:, lanes]
        total = lax.fori_loop(0, n_col // group, step, start)
        if p == 0:
            sums_ref[:, lanes] = total
        return total

    def gather(p):
        rs_recv[p, me_col] = l_ref[p, me_col]
        for peer in col_peers:
            scatter_copy(p, me_col, peer).wait_recv()
        whole = jnp.sum(rs_recv[p], axis=0)
        t_ref[p, me_col] = t_ref[p, me_col] + ((log2_a + lift) - lifted_log2(whole))
        for peer in col_peers:
            gather_copy(p, peer, me_col).start()

    def gathered(p):
        for peer in col_peers:
            gather_copy(p, me_col, peer).wait_recv()

    def col_exchange(k, h, total):
        total = jnp.sum(total, axis=0, keepdims=True)
        c_send[k, h] = total
        for peer in row_peers:
            col_copy(k, h, peer, me_row).start()
        c_recv[k, h, me_row] = total

    def col_update(k, h, last):
        lanes = pl.ds(h * half, half)
        for peer in row_peers:
            col_copy(k, h, me_row, peer).wait_recv()
        whole = jnp.sum(c_recv[k, h], axis=0)
        u_ref[:, lanes] = u_ref[:, lanes] + ((log2_b + lift) - lifted_log2(whole))
        if not last:
            b_ref[bias_rows, lanes] = with_bias(bbase[:, lanes], u_ref[:, lanes], 3).astype(
                jnp.bfloat16
            )
            bt_ref[lanes, changing] = b_ref[changing, lanes].T

    def iteration(k, carry):
        for h in range(2):

            @pl.when(k > 0)
            def _():
                col_update(k - 1, h, False)

            row_quarter(h, 0)
        row_quarter(0, 1)
        gather(0)
        row_quarter(1, 1)
        gathered(0)
        col_quarter(0, 0)
        gather(1)
        col_quarter(1, 0)
        gathered(1)
        col_exchange(k, 0, col_quarter(0, 1))
        col_exchange(k, 1, col_quarter(1, 1))
        for p in range(2):
            for peer in col_peers:
                scatter_copy(p, peer, me_col).wait_send()
                gather_copy(p, peer, me_col).wait_send()
        return carry

    lax.fori_loop(0, ITERS, iteration, 0)

    for q in range(n_col):
        for i in range(per):
            part, inner = divmod(i * block, part_width)
            inner = pl.ds(inner, block)
            f_ref[pl.ds(q * per + i, 1), :] = (
                t_ref[part, q, :, inner] + nx_ref[part, q, :, inner]
            ) * (1.0 / kappa)
    for h in range(2):
        col_update(ITERS - 1, h, True)
    flag_recv[me_col] = sum(u_ref[:, i * 128 : (i + 1) * 128] for i in range(cols // 128))
    for peer in col_peers:
        flag_copy(peer, me_col).start()
    potential = (u_ref[...] + ny_ref[...]) * (1.0 / kappa)
    for c in range(col_blocks):
        g_ref[pl.ds(c, 1), :] = potential[:, c * block : (c + 1) * block]
    for k in range(ITERS):
        for h in range(2):
            for peer in row_peers:
                col_copy(k, h, peer, me_row).wait_send()
    for peer in col_peers:
        flag_copy(me_col, peer).wait_recv()
        flag_copy(peer, me_col).wait_send()
    seen = jnp.sum(jnp.sum(flag_recv[...], axis=0), axis=1, keepdims=True)
    flag_ref[...] = jnp.broadcast_to(jnp.where(seen == seen, 0, 1), flag_ref.shape)


def run_fast(n_row, n_col, row_points, col_points, block_lists):
    row_blocks, dim, block = row_points.shape
    col_blocks = col_points.shape[0]
    width = row_blocks // n_col * block
    cols = col_blocks * block
    f32, bf16 = jnp.float32, jnp.bfloat16
    pairs = row_blocks * col_blocks * block * block
    vmem = pl.BlockSpec(memory_space=pltpu.VMEM)
    sems = pltpu.SemaphoreType.DMA
    return pl.pallas_call(
        functools.partial(fast_kernel, n_row, n_col),
        out_shape=(
            jax.ShapeDtypeStruct((row_blocks, block), f32),
            jax.ShapeDtypeStruct((col_blocks, block), f32),
            jax.ShapeDtypeStruct((1, 128), jnp.int32),
        ),
        in_specs=[vmem] * 3,
        out_specs=(vmem, vmem, vmem),
        scratch_shapes=[
            pltpu.VMEM((n_col, depth, width), bf16),
            pltpu.VMEM((n_col, width, depth), bf16),
            pltpu.VMEM((depth, cols), bf16),
            pltpu.VMEM((cols, depth), bf16),
            pltpu.VMEM((n_col, slab, width), f32),
            pltpu.VMEM((slab, cols), f32),
            pltpu.VMEM((2, n_col, 1, width // 2), f32),
            pltpu.VMEM((1, cols), f32),
            pltpu.VMEM((2, n_col, 1, width // 2), f32),
            pltpu.VMEM((1, cols), f32),
            pltpu.VMEM((2, n_col, 1, width // 2), f32),
            pltpu.VMEM((2, n_col, 1, width // 2), f32),
            pltpu.VMEM((ITERS, 2, 1, cols // 2), f32),
            pltpu.VMEM((ITERS, 2, n_row, 1, cols // 2), f32),
            pltpu.VMEM((8, cols), f32),
            pltpu.VMEM((n_col, 1, 128), f32),
            sems((2, n_col)), sems((2, n_col)), sems((2, n_col)), sems((2, n_col)),
            sems((ITERS, 2, n_row)), sems((ITERS, 2, n_row)),
            sems((n_col,)), sems((n_col,)),
        ],
        compiler_params=pltpu.CompilerParams(
            collective_id=0, has_side_effects=True, vmem_limit_bytes=40 * 1024 * 1024
        ),
        cost_estimate=pl.CostEstimate(
            flops=2 * 2 * ITERS * pairs * depth,
            bytes_accessed=row_blocks * dim * block * 2,
            transcendentals=2 * ITERS * pairs,
        ),
    )(block_lists, row_points, col_points)


def body(n_row, n_col, *arguments):
    row_potential, col_potential, flag = run_fast(n_row, n_col, *arguments)
    return lax.cond(
        flag[0, 0] > 0,
        lambda *operands: run(True, n_row, n_col, *operands[2:])[:2],
        lambda *operands: operands[:2],
        row_potential,
        col_potential,
        *arguments,
    )


def solution(mesh):
    placed = (P("row", None, None), P("col", None, None), P("row", None))
    return jax.shard_map(
        functools.partial(body, mesh.shape["row"], mesh.shape["col"]),
        mesh=mesh,
        in_specs=placed,
        out_specs=(P("row", None), P("col", None)),
        check_vma=False,
    )
```

```python
import functools
import math

import jax
import jax.numpy as jnp
from jax import lax
from jax.experimental import pallas as pl
from jax.experimental.pallas import tpu as pltpu
from jax.sharding import PartitionSpec as P

ITERS = 4
eps_reg = 0.05
kappa = math.log2(math.e) / eps_reg
masked_score = -(2.0**40)
lift = 100.0
least, most = 2.0**-80, 2.0**126
depth = 256
slab = 16
MESH = pl.DeviceIdType.MESH


def split3(values):
    high = values.astype(jnp.bfloat16).astype(jnp.float32)
    rest = values - high
    mid = rest.astype(jnp.bfloat16).astype(jnp.float32)
    low = (rest - mid).astype(jnp.bfloat16).astype(jnp.float32)
    return high, mid, low


def with_bias(base, bias, first):
    rows = lax.broadcasted_iota(jnp.int32, base.shape, 0)
    high, mid, low = split3(bias)
    out = jnp.where(rows == first, high, base)
    out = jnp.where(rows == first + 1, mid, out)
    return jnp.where(rows == first + 2, low, out)


def log2_sum(parts):
    peak = jnp.max(parts, axis=0, keepdims=True)
    return peak + jnp.log2(jnp.sum(jnp.exp2(parts - peak), axis=0, keepdims=True))


def lifted_log2(total):
    inside = (total > least) & (total < most)
    return jnp.log2(jnp.where(inside, total, jnp.nan))


def kernel(
    exact, n_row, n_col, lists_ref, x_ref, y_ref, f_ref, g_ref, flag_ref,
    a_ref, at_ref, b_ref, bt_ref, abase, bbase, t_ref, u_ref, nx_ref, ny_ref,
    l_ref, rs_recv, lc_ref, c_send, c_recv, s_ref, sums_ref, flag_recv,
    rs_ssem, rs_rsem, ag_ssem, ag_rsem, c_ssem, c_rsem, flag_ssem, flag_rsem,
):
    me_row = lax.axis_index("row")
    me_col = lax.axis_index("col")
    row_blocks, dim, block = x_ref.shape
    col_blocks = y_ref.shape[0]
    per = row_blocks // n_col
    width = per * block
    cols = col_blocks * block
    log2_a = -math.log2(n_row * row_blocks * block)
    log2_b = -math.log2(n_col * cols)
    alpha = 2.0 * kappa / dim
    beta = kappa / dim
    raise_by = 0.0 if exact else lift

    barrier = pltpu.get_barrier_semaphore()
    for step in range(1, n_col):
        pl.semaphore_signal(
            barrier, inc=1, device_id={"col": lax.rem(me_col + step, n_col)}, device_id_type=MESH
        )
    for step in range(1, n_row):
        pl.semaphore_signal(
            barrier, inc=1, device_id={"row": lax.rem(me_row + step, n_row)}, device_id_type=MESH
        )

    slab_rows = lax.broadcasted_iota(jnp.int32, (slab, block), 0)
    zeros = jnp.zeros((depth - 3 * dim - slab, block), jnp.bfloat16)

    for c in range(col_blocks):
        lanes = pl.ds(c * block, block)
        y = y_ref[c]
        for part in range(3):
            b_ref[pl.ds(part * dim, dim), lanes] = y
        y32 = y.astype(jnp.float32)
        norm = jnp.sum(y32 * y32, axis=0, keepdims=True) * beta
        ny_ref[:, lanes] = norm
        u_ref[:, lanes] = -norm
        base = jnp.where((slab_rows < 3) | (slab_rows == 6 + c), 1.0, 0.0)
        bbase[:, lanes] = base
        b_ref[pl.ds(3 * dim, slab), lanes] = with_bias(base, -norm, 3).astype(jnp.bfloat16)
        b_ref[pl.ds(3 * dim + slab, depth - 3 * dim - slab), lanes] = zeros
        bt_ref[pl.ds(c * block, block), :] = b_ref[:, lanes].T

    def prepare(q, carry):
        for part in range(per):
            r = q * per + part
            lanes = pl.ds(part * block, block)
            x = x_ref[r].astype(jnp.float32)
            norm = jnp.sum(x * x, axis=0, keepdims=True) * beta
            nx_ref[q, :, lanes] = norm
            t_ref[q, :, lanes] = -norm
            for i, piece in enumerate(split3(x * alpha)):
                a_ref[q, pl.ds(i * dim, dim), lanes] = piece.astype(jnp.bfloat16)
            listed = lists_ref[pl.ds(r, 1), :]
            base = jnp.where((slab_rows >= 3) & (slab_rows < 6), 1.0, 0.0)
            for c in range(col_blocks):
                hit = jnp.where(listed == me_col * col_blocks + c, 1.0, 0.0)
                hit = jnp.max(hit, axis=1, keepdims=True)
                fill = jnp.broadcast_to(jnp.where(hit > 0.0, 0.0, masked_score), (slab, block))
                base = jnp.where(slab_rows == 6 + c, fill, base)
            abase[q, :, lanes] = base
            a_ref[q, pl.ds(3 * dim, slab), lanes] = with_bias(base, raise_by - norm, 0).astype(jnp.bfloat16)
            a_ref[q, pl.ds(3 * dim + slab, depth - 3 * dim - slab), lanes] = zeros
            at_ref[q, pl.ds(part * block, block), :] = a_ref[q, :, lanes].T
        return carry

    lax.fori_loop(0, n_col, prepare, 0)
    pl.semaphore_wait(barrier, n_col - 1 + n_row - 1)

    def row_part(q):
        points = a_ref[q]
        if not exact:
            total = jnp.zeros((8, width), jnp.float32)
            for c in range(col_blocks):
                scores = jnp.dot(
                    bt_ref[pl.ds(c * block, block), :], points, preferred_element_type=jnp.float32
                )
                total += jnp.sum(jnp.exp2(scores).reshape(block // 8, 8, width), axis=0)
            return jnp.sum(total, axis=0, keepdims=True)
        peak = None
        for c in range(col_blocks):
            scores = jnp.dot(
                bt_ref[pl.ds(c * block, block), :], points, preferred_element_type=jnp.float32
            )
            s_ref[c] = scores
            top = jnp.max(scores.reshape(block // 8, 8, width), axis=0)
            peak = top if peak is None else jnp.maximum(peak, top)
        peak = jnp.max(peak, axis=0, keepdims=True)
        total = jnp.zeros((8, width), jnp.float32)
        for c in range(col_blocks):
            total += jnp.sum(jnp.exp2(s_ref[c] - peak).reshape(block // 8, 8, width), axis=0)
        return peak + jnp.log2(jnp.sum(total, axis=0, keepdims=True))

    def scatter_copy(peer, slot):
        return pltpu.make_async_remote_copy(
            src_ref=l_ref.at[peer], dst_ref=rs_recv.at[slot],
            send_sem=rs_ssem.at[peer], recv_sem=rs_rsem.at[slot],
            device_id={"col": peer}, device_id_type=MESH,
        )

    def gather_copy(peer, slot):
        return pltpu.make_async_remote_copy(
            src_ref=t_ref.at[slot], dst_ref=t_ref.at[slot],
            send_sem=ag_ssem.at[peer], recv_sem=ag_rsem.at[slot],
            device_id={"col": peer}, device_id_type=MESH,
        )

    def col_copy(peer, slot, k):
        return pltpu.make_async_remote_copy(
            src_ref=c_send.at[k], dst_ref=c_recv.at[k, slot],
            send_sem=c_ssem.at[k, peer], recv_sem=c_rsem.at[k, slot],
            device_id={"row": peer}, device_id_type=MESH,
        )

    def combined(parts):
        if exact:
            return log2_sum(parts)[0]
        return lifted_log2(jnp.sum(parts, axis=0))

    def iteration(k, carry):
        def row_step(s, c2):
            q = lax.rem(me_col + 1 + s, n_col)
            l_ref[q] = row_part(q)

            @pl.when(s < n_col - 1)
            def _():
                scatter_copy(q, me_col).start()

            return c2

        lax.fori_loop(0, n_col, row_step, 0)
        rs_recv[me_col] = l_ref[me_col]

        def row_wait(s, c2):
            scatter_copy(me_col, lax.rem(me_col + 1 + s, n_col)).wait_recv()
            return c2

        lax.fori_loop(0, n_col - 1, row_wait, 0)
        t_ref[me_col] = t_ref[me_col] + ((log2_a + raise_by) - combined(rs_recv[...]))

        def row_send(s, c2):
            gather_copy(lax.rem(me_col + 1 + s, n_col), me_col).start()
            return c2

        lax.fori_loop(0, n_col - 1, row_send, 0)

        def col_step(s, c2):
            q = lax.rem(me_col + s, n_col)

            @pl.when(s > 0)
            def _():
                gather_copy(me_col, q).wait_recv()

            a_ref[q, pl.ds(3 * dim, slab), :] = with_bias(abase[q], t_ref[q] + raise_by, 0).astype(
                jnp.bfloat16
            )
            at_ref[q, :, pl.ds(depth // 2, depth // 2)] = a_ref[
                q, pl.ds(depth // 2, depth // 2), :
            ].T
            points = at_ref[q]
            for c in range(col_blocks):
                lanes = pl.ds(c * block, block)
                scores = jnp.dot(points, b_ref[:, lanes], preferred_element_type=jnp.float32)
                if exact:
                    peak = jnp.max(scores, axis=0, keepdims=True)
                    total = jnp.sum(jnp.exp2(scores - peak), axis=0, keepdims=True)
                    lc_ref[q, :, lanes] = peak + jnp.log2(total)
                else:
                    sums_ref[:, lanes] += jnp.sum(
                        jnp.exp2(scores).reshape(width // 8, 8, block), axis=0
                    )
            return c2

        sums_ref[...] = jnp.zeros((8, cols), jnp.float32)
        lax.fori_loop(0, n_col, col_step, 0)
        if exact:
            c_send[k] = log2_sum(lc_ref[...])[0]
        else:
            c_send[k] = jnp.sum(sums_ref[...], axis=0, keepdims=True)

        def col_send(s, c2):
            col_copy(lax.rem(me_row + 1 + s, n_row), me_row, k).start()
            return c2

        lax.fori_loop(0, n_row - 1, col_send, 0)
        c_recv[k, me_row] = c_send[k]

        def row_done(s, c2):
            peer = lax.rem(me_col + 1 + s, n_col)
            scatter_copy(peer, me_col).wait_send()
            gather_copy(peer, me_col).wait_send()
            return c2

        lax.fori_loop(0, n_col - 1, row_done, 0)

        def col_wait(s, c2):
            col_copy(me_row, lax.rem(me_row + 1 + s, n_row), k).wait_recv()
            return c2

        lax.fori_loop(0, n_row - 1, col_wait, 0)
        u_ref[...] = u_ref[...] + ((log2_b + raise_by) - combined(c_recv[k]))
        b_ref[pl.ds(3 * dim, slab), :] = with_bias(bbase[...], u_ref[...], 3).astype(jnp.bfloat16)
        bt_ref[:, pl.ds(depth // 2, depth // 2)] = b_ref[pl.ds(depth // 2, depth // 2), :].T
        return carry

    lax.fori_loop(0, ITERS, iteration, 0)

    def flag_copy(peer, slot):
        return pltpu.make_async_remote_copy(
            src_ref=flag_recv.at[slot], dst_ref=flag_recv.at[slot],
            send_sem=flag_ssem.at[peer], recv_sem=flag_rsem.at[slot],
            device_id={"col": peer}, device_id_type=MESH,
        )

    def flag_send(s, carry):
        flag_copy(lax.rem(me_col + 1 + s, n_col), me_col).start()
        return carry

    def flag_wait(s, carry):
        peer = lax.rem(me_col + 1 + s, n_col)
        flag_copy(me_col, peer).wait_recv()
        flag_copy(peer, me_col).wait_send()
        return carry

    if not exact:
        flag_recv[me_col] = sum(u_ref[:, i * 128 : (i + 1) * 128] for i in range(cols // 128))
        lax.fori_loop(0, n_col - 1, flag_send, 0)

    for q in range(n_col):
        potential = (t_ref[q] + nx_ref[q]) * (1.0 / kappa)
        for part in range(per):
            f_ref[pl.ds(q * per + part, 1), :] = potential[:, part * block : (part + 1) * block]
    potential = (u_ref[...] + ny_ref[...]) * (1.0 / kappa)
    for c in range(col_blocks):
        g_ref[pl.ds(c, 1), :] = potential[:, c * block : (c + 1) * block]

    def col_done(i, carry):
        peer = lax.rem(me_row + 1 + lax.rem(i, n_row - 1), n_row)
        col_copy(peer, me_row, i // (n_row - 1)).wait_send()
        return carry

    lax.fori_loop(0, ITERS * (n_row - 1), col_done, 0)
    if exact:
        flag_ref[...] = jnp.zeros_like(flag_ref)
    else:
        lax.fori_loop(0, n_col - 1, flag_wait, 0)
        seen = jnp.sum(jnp.sum(flag_recv[...], axis=0), axis=1, keepdims=True)
        flag_ref[...] = jnp.broadcast_to(jnp.where(seen == seen, 0, 1), flag_ref.shape)


def run(exact, n_row, n_col, row_points, col_points, block_lists):
    row_blocks, dim, block = row_points.shape
    col_blocks = col_points.shape[0]
    width = row_blocks // n_col * block
    cols = col_blocks * block
    f32, bf16 = jnp.float32, jnp.bfloat16
    pairs = row_blocks * col_blocks * block * block
    vmem = pl.BlockSpec(memory_space=pltpu.VMEM)
    return pl.pallas_call(
        functools.partial(kernel, exact, n_row, n_col),
        out_shape=(
            jax.ShapeDtypeStruct((row_blocks, block), f32),
            jax.ShapeDtypeStruct((col_blocks, block), f32),
            jax.ShapeDtypeStruct((1, 128), jnp.int32),
        ),
        in_specs=[vmem] * 3,
        out_specs=(vmem, vmem, vmem),
        scratch_shapes=[
            pltpu.VMEM((n_col, depth, width), bf16),
            pltpu.VMEM((n_col, width, depth), bf16),
            pltpu.VMEM((depth, cols), bf16),
            pltpu.VMEM((cols, depth), bf16),
            pltpu.VMEM((n_col, slab, width), f32),
            pltpu.VMEM((slab, cols), f32),
            pltpu.VMEM((n_col, 1, width), f32),
            pltpu.VMEM((1, cols), f32),
            pltpu.VMEM((n_col, 1, width), f32),
            pltpu.VMEM((1, cols), f32),
            pltpu.VMEM((n_col, 1, width), f32),
            pltpu.VMEM((n_col, 1, width), f32),
            pltpu.VMEM((n_col, 1, cols), f32),
            pltpu.VMEM((ITERS, 1, cols), f32),
            pltpu.VMEM((ITERS, n_row, 1, cols), f32),
            pltpu.VMEM((col_blocks, block, width) if exact else (1, 8, 128), f32),
            pltpu.VMEM((8, cols), f32),
            pltpu.VMEM((n_col, 1, 128), f32),
            pltpu.SemaphoreType.DMA((n_col,)),
            pltpu.SemaphoreType.DMA((n_col,)),
            pltpu.SemaphoreType.DMA((n_col,)),
            pltpu.SemaphoreType.DMA((n_col,)),
            pltpu.SemaphoreType.DMA((ITERS, n_row)),
            pltpu.SemaphoreType.DMA((ITERS, n_row)),
            pltpu.SemaphoreType.DMA((n_col,)),
            pltpu.SemaphoreType.DMA((n_col,)),
        ],
        compiler_params=pltpu.CompilerParams(
            collective_id=int(exact), has_side_effects=True, vmem_limit_bytes=56 * 1024 * 1024
        ),
        cost_estimate=pl.CostEstimate(
            flops=2 * 2 * ITERS * pairs * depth,
            bytes_accessed=row_blocks * dim * block * 2,
            transcendentals=2 * ITERS * pairs,
        ),
    )(block_lists, row_points, col_points)


def fast_kernel(
    n_row, n_col, lists_ref, x_ref, y_ref, f_ref, g_ref, flag_ref,
    a_ref, b_ref, bt_ref, abase, bbase, t_ref, u_ref, nx_ref, ny_ref,
    l_ref, rs_recv, c_send, c_recv, sums_ref, flag_recv,
    rs_ssem, rs_rsem, ag_ssem, ag_rsem, c_ssem, c_rsem, flag_ssem, flag_rsem,
):
    me_row = lax.axis_index("row")
    me_col = lax.axis_index("col")
    row_blocks, dim, block = x_ref.shape
    col_blocks = y_ref.shape[0]
    per = row_blocks // n_col
    width = per * block
    cols = col_blocks * block
    log2_a = -math.log2(n_row * row_blocks * block)
    log2_b = -math.log2(n_col * cols)
    alpha = 2.0 * kappa / dim
    beta = kappa / dim
    bias_rows = pl.ds(3 * dim, slab)
    spare_rows = pl.ds(3 * dim + slab, depth - 3 * dim - slab)
    changing = pl.ds(depth // 2, depth // 2)

    barrier = pltpu.get_barrier_semaphore()
    for step in range(1, n_col):
        pl.semaphore_signal(
            barrier, inc=1, device_id={"col": lax.rem(me_col + step, n_col)}, device_id_type=MESH
        )
    for step in range(1, n_row):
        pl.semaphore_signal(
            barrier, inc=1, device_id={"row": lax.rem(me_row + step, n_row)}, device_id_type=MESH
        )

    slab_rows = lax.broadcasted_iota(jnp.int32, (slab, block), 0)
    zeros = jnp.zeros((depth - 3 * dim - slab, block), jnp.bfloat16)

    for c in range(col_blocks):
        lanes = pl.ds(c * block, block)
        y = y_ref[c]
        for part in range(3):
            b_ref[pl.ds(part * dim, dim), lanes] = y
        y32 = y.astype(jnp.float32)
        norm = jnp.sum(y32 * y32, axis=0, keepdims=True) * beta
        ny_ref[:, lanes] = norm
        u_ref[:, lanes] = -norm
        base = jnp.where((slab_rows < 3) | (slab_rows == 6 + c), 1.0, 0.0)
        bbase[:, lanes] = base
        b_ref[bias_rows, lanes] = with_bias(base, -norm, 3).astype(jnp.bfloat16)
        b_ref[spare_rows, lanes] = zeros
        bt_ref[pl.ds(c * block, block), :] = b_ref[:, lanes].T

    def prepare(q, carry):
        for i in range(per):
            r = q * per + i
            lanes = pl.ds(i * block, block)
            x = x_ref[r].astype(jnp.float32)
            norm = jnp.sum(x * x, axis=0, keepdims=True) * beta
            nx_ref[q, :, lanes] = norm
            t_ref[q, :, lanes] = -norm
            for j, piece in enumerate(split3(x * alpha)):
                a_ref[q, pl.ds(j * dim, dim), lanes] = piece.astype(jnp.bfloat16)
            listed = lists_ref[pl.ds(r, 1), :]
            base = jnp.where((slab_rows >= 3) & (slab_rows < 6), 1.0, 0.0)
            for c in range(col_blocks):
                hit = jnp.where(listed == me_col * col_blocks + c, 1.0, 0.0)
                hit = jnp.max(hit, axis=1, keepdims=True)
                fill = jnp.broadcast_to(jnp.where(hit > 0.0, 0.0, masked_score), (slab, block))
                base = jnp.where(slab_rows == 6 + c, fill, base)
            abase[q, :, lanes] = base
            a_ref[q, bias_rows, lanes] = with_bias(base, lift - norm, 0).astype(jnp.bfloat16)
            a_ref[q, spare_rows, lanes] = zeros
        return carry

    lax.fori_loop(0, n_col, prepare, 0)
    pl.semaphore_wait(barrier, n_col - 1 + n_row - 1)

    def scatter_copy(peer):
        return pltpu.make_async_remote_copy(
            src_ref=l_ref.at[peer], dst_ref=rs_recv.at[me_col],
            send_sem=rs_ssem, recv_sem=rs_rsem,
            device_id={"col": peer}, device_id_type=MESH,
        )

    def gather_copy(peer):
        return pltpu.make_async_remote_copy(
            src_ref=t_ref.at[me_col], dst_ref=t_ref.at[me_col],
            send_sem=ag_ssem, recv_sem=ag_rsem,
            device_id={"col": peer}, device_id_type=MESH,
        )

    def col_copy(k, peer):
        return pltpu.make_async_remote_copy(
            src_ref=c_send.at[k], dst_ref=c_recv.at[k, me_row],
            send_sem=c_ssem.at[k], recv_sem=c_rsem.at[k],
            device_id={"row": peer}, device_id_type=MESH,
        )

    def flag_copy(peer):
        return pltpu.make_async_remote_copy(
            src_ref=flag_recv.at[me_col], dst_ref=flag_recv.at[me_col],
            send_sem=flag_ssem, recv_sem=flag_rsem,
            device_id={"col": peer}, device_id_type=MESH,
        )

    def wait_all(ref, peers, sem):
        some = ref.at[pl.ds(0, peers)]
        pltpu.make_async_copy(some, some, sem).wait()

    col_peers = [lax.rem(me_col + step, n_col) for step in range(1, n_col)]
    row_peers = [lax.rem(me_row + step, n_row) for step in range(1, n_row)]

    def exponentials(q, i):
        scores = jnp.dot(
            bt_ref[...], a_ref[q, :, pl.ds(i * block, block)], preferred_element_type=jnp.float32
        )
        return jnp.exp2(scores)

    def row_part(q):
        for i in range(per):
            total = jnp.sum(exponentials(q, i).reshape(cols // 8, 8, block), axis=0)
            l_ref[q, :, pl.ds(i * block, block)] = jnp.sum(total, axis=0, keepdims=True)

    def col_part(q):
        a_ref[q, bias_rows, :] = with_bias(abase[q], t_ref[q] + lift, 0).astype(jnp.bfloat16)
        for i in range(per):
            terms = exponentials(q, i)
            sums_ref[...] += sum(terms[:, j : j + 128] for j in range(0, block, 128))

    def iteration(k, carry):
        def row_step(s, c2):
            q = lax.rem(me_col + 1 + s, n_col)
            row_part(q)
            scatter_copy(q).start()
            return c2

        lax.fori_loop(0, n_col - 1, row_step, 0)
        row_part(me_col)
        rs_recv[me_col] = l_ref[me_col]
        wait_all(rs_recv, n_col - 1, rs_rsem)
        whole = jnp.sum(rs_recv[...], axis=0)
        t_ref[me_col] = t_ref[me_col] + ((log2_a + lift) - lifted_log2(whole))
        for peer in col_peers:
            gather_copy(peer).start()

        sums_ref[...] = jnp.zeros((cols, 128), jnp.float32)
        col_part(me_col)
        wait_all(t_ref, n_col - 1, ag_rsem)

        def col_step(s, c2):
            col_part(lax.rem(me_col + 1 + s, n_col))
            return c2

        lax.fori_loop(0, n_col - 1, col_step, 0)
        share = jnp.sum(sums_ref[...].T, axis=0, keepdims=True)
        c_send[k] = share
        for peer in row_peers:
            col_copy(k, peer).start()
        c_recv[k, me_row] = share
        wait_all(l_ref, n_col - 1, rs_ssem)
        wait_all(t_ref, n_col - 1, ag_ssem)
        wait_all(c_recv.at[k], n_row - 1, c_rsem.at[k])
        whole = jnp.sum(c_recv[k], axis=0)
        u_ref[...] = u_ref[...] + ((log2_b + lift) - lifted_log2(whole))
        b_ref[bias_rows, :] = with_bias(bbase[...], u_ref[...], 3).astype(jnp.bfloat16)
        bt_ref[:, changing] = b_ref[changing, :].T
        return carry

    lax.fori_loop(0, ITERS, iteration, 0)

    for q in range(n_col):
        for i in range(per):
            lanes = pl.ds(i * block, block)
            f_ref[pl.ds(q * per + i, 1), :] = (t_ref[q, :, lanes] + nx_ref[q, :, lanes]) * (
                1.0 / kappa
            )
    flag_recv[me_col] = sum(u_ref[:, i * 128 : (i + 1) * 128] for i in range(cols // 128))
    for peer in col_peers:
        flag_copy(peer).start()
    potential = (u_ref[...] + ny_ref[...]) * (1.0 / kappa)
    for c in range(col_blocks):
        g_ref[pl.ds(c, 1), :] = potential[:, c * block : (c + 1) * block]
    for k in range(ITERS):
        wait_all(c_recv.at[k], n_row - 1, c_ssem.at[k])
    wait_all(flag_recv, n_col - 1, flag_rsem)
    wait_all(flag_recv, n_col - 1, flag_ssem)
    seen = jnp.sum(jnp.sum(flag_recv[...], axis=0), axis=1, keepdims=True)
    flag_ref[...] = jnp.broadcast_to(jnp.where(seen == seen, 0, 1), flag_ref.shape)


def run_fast(n_row, n_col, row_points, col_points, block_lists):
    row_blocks, dim, block = row_points.shape
    col_blocks = col_points.shape[0]
    width = row_blocks // n_col * block
    cols = col_blocks * block
    f32, bf16 = jnp.float32, jnp.bfloat16
    pairs = row_blocks * col_blocks * block * block
    vmem = pl.BlockSpec(memory_space=pltpu.VMEM)
    sems = pltpu.SemaphoreType.DMA
    return pl.pallas_call(
        functools.partial(fast_kernel, n_row, n_col),
        out_shape=(
            jax.ShapeDtypeStruct((row_blocks, block), f32),
            jax.ShapeDtypeStruct((col_blocks, block), f32),
            jax.ShapeDtypeStruct((1, 128), jnp.int32),
        ),
        in_specs=[vmem] * 3,
        out_specs=(vmem, vmem, vmem),
        scratch_shapes=[
            pltpu.VMEM((n_col, depth, width), bf16),
            pltpu.VMEM((depth, cols), bf16),
            pltpu.VMEM((cols, depth), bf16),
            pltpu.VMEM((n_col, slab, width), f32),
            pltpu.VMEM((slab, cols), f32),
            pltpu.VMEM((n_col, 1, width), f32),
            pltpu.VMEM((1, cols), f32),
            pltpu.VMEM((n_col, 1, width), f32),
            pltpu.VMEM((1, cols), f32),
            pltpu.VMEM((n_col, 1, width), f32),
            pltpu.VMEM((n_col, 1, width), f32),
            pltpu.VMEM((ITERS, 1, cols), f32),
            pltpu.VMEM((ITERS, n_row, 1, cols), f32),
            pltpu.VMEM((cols, 128), f32),
            pltpu.VMEM((n_col, 1, 128), f32),
            sems, sems, sems, sems,
            sems((ITERS,)), sems((ITERS,)),
            sems, sems,
        ],
        compiler_params=pltpu.CompilerParams(
            collective_id=0, has_side_effects=True, vmem_limit_bytes=40 * 1024 * 1024
        ),
        cost_estimate=pl.CostEstimate(
            flops=2 * 2 * ITERS * pairs * depth,
            bytes_accessed=row_blocks * dim * block * 2,
            transcendentals=2 * ITERS * pairs,
        ),
    )(block_lists, row_points, col_points)


def body(n_row, n_col, *arguments):
    row_potential, col_potential, flag = run_fast(n_row, n_col, *arguments)
    return lax.cond(
        flag[0, 0] > 0,
        lambda *operands: run(True, n_row, n_col, *operands[2:])[:2],
        lambda *operands: operands[:2],
        row_potential,
        col_potential,
        *arguments,
    )


def solution(mesh):
    placed = (P("row", None, None), P("col", None, None), P("row", None))
    return jax.shard_map(
        functools.partial(body, mesh.shape["row"], mesh.shape["col"]),
        mesh=mesh,
        in_specs=placed,
        out_specs=(P("row", None), P("col", None)),
        check_vma=False,
    )
```

```python
import functools
import math

import jax
import jax.numpy as jnp
from jax import lax
from jax.experimental import pallas as pl
from jax.experimental.pallas import tpu as pltpu
from jax.sharding import PartitionSpec as P

ITERS = 4
eps_reg = 0.05
kappa = math.log2(math.e) / eps_reg
masked_score = -(2.0**40)
lift = 100.0
least, most = 2.0**-80, 2.0**126
depth = 256
shallow = 128
slab = 16
MESH = pl.DeviceIdType.MESH


def split3(values):
    high = values.astype(jnp.bfloat16).astype(jnp.float32)
    rest = values - high
    mid = rest.astype(jnp.bfloat16).astype(jnp.float32)
    low = (rest - mid).astype(jnp.bfloat16).astype(jnp.float32)
    return high, mid, low


def with_bias(base, bias, first):
    rows = lax.broadcasted_iota(jnp.int32, base.shape, 0)
    high, mid, low = split3(bias)
    out = jnp.where(rows == first, high, base)
    out = jnp.where(rows == first + 1, mid, out)
    return jnp.where(rows == first + 2, low, out)


def log2_sum(parts):
    peak = jnp.max(parts, axis=0, keepdims=True)
    return peak + jnp.log2(jnp.sum(jnp.exp2(parts - peak), axis=0, keepdims=True))


def lifted_log2(total):
    inside = (total > least) & (total < most)
    return jnp.log2(jnp.where(inside, total, jnp.nan))


def kernel(
    exact, n_row, n_col, lists_ref, x_ref, y_ref, f_ref, g_ref, flag_ref,
    a_ref, at_ref, b_ref, bt_ref, abase, bbase, t_ref, u_ref, nx_ref, ny_ref,
    l_ref, rs_recv, lc_ref, c_send, c_recv, s_ref, sums_ref, flag_recv,
    rs_ssem, rs_rsem, ag_ssem, ag_rsem, c_ssem, c_rsem, flag_ssem, flag_rsem,
):
    me_row = lax.axis_index("row")
    me_col = lax.axis_index("col")
    row_blocks, dim, block = x_ref.shape
    col_blocks = y_ref.shape[0]
    per = row_blocks // n_col
    width = per * block
    cols = col_blocks * block
    log2_a = -math.log2(n_row * row_blocks * block)
    log2_b = -math.log2(n_col * cols)
    alpha = 2.0 * kappa / dim
    beta = kappa / dim
    raise_by = 0.0 if exact else lift

    barrier = pltpu.get_barrier_semaphore()
    for step in range(1, n_col):
        pl.semaphore_signal(
            barrier, inc=1, device_id={"col": lax.rem(me_col + step, n_col)}, device_id_type=MESH
        )
    for step in range(1, n_row):
        pl.semaphore_signal(
            barrier, inc=1, device_id={"row": lax.rem(me_row + step, n_row)}, device_id_type=MESH
        )

    slab_rows = lax.broadcasted_iota(jnp.int32, (slab, block), 0)
    zeros = jnp.zeros((depth - 3 * dim - slab, block), jnp.bfloat16)

    for c in range(col_blocks):
        lanes = pl.ds(c * block, block)
        y = y_ref[c]
        for part in range(3):
            b_ref[pl.ds(part * dim, dim), lanes] = y
        y32 = y.astype(jnp.float32)
        norm = jnp.sum(y32 * y32, axis=0, keepdims=True) * beta
        ny_ref[:, lanes] = norm
        u_ref[:, lanes] = -norm
        base = jnp.where((slab_rows < 3) | (slab_rows == 6 + c), 1.0, 0.0)
        bbase[:, lanes] = base
        b_ref[pl.ds(3 * dim, slab), lanes] = with_bias(base, -norm, 3).astype(jnp.bfloat16)
        b_ref[pl.ds(3 * dim + slab, depth - 3 * dim - slab), lanes] = zeros
        bt_ref[pl.ds(c * block, block), :] = b_ref[:, lanes].T

    def prepare(q, carry):
        for part in range(per):
            r = q * per + part
            lanes = pl.ds(part * block, block)
            x = x_ref[r].astype(jnp.float32)
            norm = jnp.sum(x * x, axis=0, keepdims=True) * beta
            nx_ref[q, :, lanes] = norm
            t_ref[q, :, lanes] = -norm
            for i, piece in enumerate(split3(x * alpha)):
                a_ref[q, pl.ds(i * dim, dim), lanes] = piece.astype(jnp.bfloat16)
            listed = lists_ref[pl.ds(r, 1), :]
            base = jnp.where((slab_rows >= 3) & (slab_rows < 6), 1.0, 0.0)
            for c in range(col_blocks):
                hit = jnp.where(listed == me_col * col_blocks + c, 1.0, 0.0)
                hit = jnp.max(hit, axis=1, keepdims=True)
                fill = jnp.broadcast_to(jnp.where(hit > 0.0, 0.0, masked_score), (slab, block))
                base = jnp.where(slab_rows == 6 + c, fill, base)
            abase[q, :, lanes] = base
            a_ref[q, pl.ds(3 * dim, slab), lanes] = with_bias(base, raise_by - norm, 0).astype(jnp.bfloat16)
            a_ref[q, pl.ds(3 * dim + slab, depth - 3 * dim - slab), lanes] = zeros
            at_ref[q, pl.ds(part * block, block), :] = a_ref[q, :, lanes].T
        return carry

    lax.fori_loop(0, n_col, prepare, 0)
    pl.semaphore_wait(barrier, n_col - 1 + n_row - 1)

    def row_part(q):
        points = a_ref[q]
        if not exact:
            total = jnp.zeros((8, width), jnp.float32)
            for c in range(col_blocks):
                scores = jnp.dot(
                    bt_ref[pl.ds(c * block, block), :], points, preferred_element_type=jnp.float32
                )
                total += jnp.sum(jnp.exp2(scores).reshape(block // 8, 8, width), axis=0)
            return jnp.sum(total, axis=0, keepdims=True)
        peak = None
        for c in range(col_blocks):
            scores = jnp.dot(
                bt_ref[pl.ds(c * block, block), :], points, preferred_element_type=jnp.float32
            )
            s_ref[c] = scores
            top = jnp.max(scores.reshape(block // 8, 8, width), axis=0)
            peak = top if peak is None else jnp.maximum(peak, top)
        peak = jnp.max(peak, axis=0, keepdims=True)
        total = jnp.zeros((8, width), jnp.float32)
        for c in range(col_blocks):
            total += jnp.sum(jnp.exp2(s_ref[c] - peak).reshape(block // 8, 8, width), axis=0)
        return peak + jnp.log2(jnp.sum(total, axis=0, keepdims=True))

    def scatter_copy(peer, slot):
        return pltpu.make_async_remote_copy(
            src_ref=l_ref.at[peer], dst_ref=rs_recv.at[slot],
            send_sem=rs_ssem.at[peer], recv_sem=rs_rsem.at[slot],
            device_id={"col": peer}, device_id_type=MESH,
        )

    def gather_copy(peer, slot):
        return pltpu.make_async_remote_copy(
            src_ref=t_ref.at[slot], dst_ref=t_ref.at[slot],
            send_sem=ag_ssem.at[peer], recv_sem=ag_rsem.at[slot],
            device_id={"col": peer}, device_id_type=MESH,
        )

    def col_copy(peer, slot, k):
        return pltpu.make_async_remote_copy(
            src_ref=c_send.at[k], dst_ref=c_recv.at[k, slot],
            send_sem=c_ssem.at[k, peer], recv_sem=c_rsem.at[k, slot],
            device_id={"row": peer}, device_id_type=MESH,
        )

    def combined(parts):
        if exact:
            return log2_sum(parts)[0]
        return lifted_log2(jnp.sum(parts, axis=0))

    def iteration(k, carry):
        def row_step(s, c2):
            q = lax.rem(me_col + 1 + s, n_col)
            l_ref[q] = row_part(q)

            @pl.when(s < n_col - 1)
            def _():
                scatter_copy(q, me_col).start()

            return c2

        lax.fori_loop(0, n_col, row_step, 0)
        rs_recv[me_col] = l_ref[me_col]

        def row_wait(s, c2):
            scatter_copy(me_col, lax.rem(me_col + 1 + s, n_col)).wait_recv()
            return c2

        lax.fori_loop(0, n_col - 1, row_wait, 0)
        t_ref[me_col] = t_ref[me_col] + ((log2_a + raise_by) - combined(rs_recv[...]))

        def row_send(s, c2):
            gather_copy(lax.rem(me_col + 1 + s, n_col), me_col).start()
            return c2

        lax.fori_loop(0, n_col - 1, row_send, 0)

        def col_step(s, c2):
            q = lax.rem(me_col + s, n_col)

            @pl.when(s > 0)
            def _():
                gather_copy(me_col, q).wait_recv()

            a_ref[q, pl.ds(3 * dim, slab), :] = with_bias(abase[q], t_ref[q] + raise_by, 0).astype(
                jnp.bfloat16
            )
            at_ref[q, :, pl.ds(depth // 2, depth // 2)] = a_ref[
                q, pl.ds(depth // 2, depth // 2), :
            ].T
            points = at_ref[q]
            for c in range(col_blocks):
                lanes = pl.ds(c * block, block)
                scores = jnp.dot(points, b_ref[:, lanes], preferred_element_type=jnp.float32)
                if exact:
                    peak = jnp.max(scores, axis=0, keepdims=True)
                    total = jnp.sum(jnp.exp2(scores - peak), axis=0, keepdims=True)
                    lc_ref[q, :, lanes] = peak + jnp.log2(total)
                else:
                    sums_ref[:, lanes] += jnp.sum(
                        jnp.exp2(scores).reshape(width // 8, 8, block), axis=0
                    )
            return c2

        sums_ref[...] = jnp.zeros((8, cols), jnp.float32)
        lax.fori_loop(0, n_col, col_step, 0)
        if exact:
            c_send[k] = log2_sum(lc_ref[...])[0]
        else:
            c_send[k] = jnp.sum(sums_ref[...], axis=0, keepdims=True)

        def col_send(s, c2):
            col_copy(lax.rem(me_row + 1 + s, n_row), me_row, k).start()
            return c2

        lax.fori_loop(0, n_row - 1, col_send, 0)
        c_recv[k, me_row] = c_send[k]

        def row_done(s, c2):
            peer = lax.rem(me_col + 1 + s, n_col)
            scatter_copy(peer, me_col).wait_send()
            gather_copy(peer, me_col).wait_send()
            return c2

        lax.fori_loop(0, n_col - 1, row_done, 0)

        def col_wait(s, c2):
            col_copy(me_row, lax.rem(me_row + 1 + s, n_row), k).wait_recv()
            return c2

        lax.fori_loop(0, n_row - 1, col_wait, 0)
        u_ref[...] = u_ref[...] + ((log2_b + raise_by) - combined(c_recv[k]))
        b_ref[pl.ds(3 * dim, slab), :] = with_bias(bbase[...], u_ref[...], 3).astype(jnp.bfloat16)
        bt_ref[:, pl.ds(depth // 2, depth // 2)] = b_ref[pl.ds(depth // 2, depth // 2), :].T
        return carry

    lax.fori_loop(0, ITERS, iteration, 0)

    def flag_copy(peer, slot):
        return pltpu.make_async_remote_copy(
            src_ref=flag_recv.at[slot], dst_ref=flag_recv.at[slot],
            send_sem=flag_ssem.at[peer], recv_sem=flag_rsem.at[slot],
            device_id={"col": peer}, device_id_type=MESH,
        )

    def flag_send(s, carry):
        flag_copy(lax.rem(me_col + 1 + s, n_col), me_col).start()
        return carry

    def flag_wait(s, carry):
        peer = lax.rem(me_col + 1 + s, n_col)
        flag_copy(me_col, peer).wait_recv()
        flag_copy(peer, me_col).wait_send()
        return carry

    if not exact:
        flag_recv[me_col] = sum(u_ref[:, i * 128 : (i + 1) * 128] for i in range(cols // 128))
        lax.fori_loop(0, n_col - 1, flag_send, 0)

    for q in range(n_col):
        potential = (t_ref[q] + nx_ref[q]) * (1.0 / kappa)
        for part in range(per):
            f_ref[pl.ds(q * per + part, 1), :] = potential[:, part * block : (part + 1) * block]
    potential = (u_ref[...] + ny_ref[...]) * (1.0 / kappa)
    for c in range(col_blocks):
        g_ref[pl.ds(c, 1), :] = potential[:, c * block : (c + 1) * block]

    def col_done(i, carry):
        peer = lax.rem(me_row + 1 + lax.rem(i, n_row - 1), n_row)
        col_copy(peer, me_row, i // (n_row - 1)).wait_send()
        return carry

    lax.fori_loop(0, ITERS * (n_row - 1), col_done, 0)
    if exact:
        flag_ref[...] = jnp.zeros_like(flag_ref)
    else:
        lax.fori_loop(0, n_col - 1, flag_wait, 0)
        seen = jnp.sum(jnp.sum(flag_recv[...], axis=0), axis=1, keepdims=True)
        flag_ref[...] = jnp.broadcast_to(jnp.where(seen == seen, 0, 1), flag_ref.shape)


def run(exact, n_row, n_col, row_points, col_points, block_lists):
    row_blocks, dim, block = row_points.shape
    col_blocks = col_points.shape[0]
    width = row_blocks // n_col * block
    cols = col_blocks * block
    f32, bf16 = jnp.float32, jnp.bfloat16
    pairs = row_blocks * col_blocks * block * block
    vmem = pl.BlockSpec(memory_space=pltpu.VMEM)
    return pl.pallas_call(
        functools.partial(kernel, exact, n_row, n_col),
        out_shape=(
            jax.ShapeDtypeStruct((row_blocks, block), f32),
            jax.ShapeDtypeStruct((col_blocks, block), f32),
            jax.ShapeDtypeStruct((1, 128), jnp.int32),
        ),
        in_specs=[vmem] * 3,
        out_specs=(vmem, vmem, vmem),
        scratch_shapes=[
            pltpu.VMEM((n_col, depth, width), bf16),
            pltpu.VMEM((n_col, width, depth), bf16),
            pltpu.VMEM((depth, cols), bf16),
            pltpu.VMEM((cols, depth), bf16),
            pltpu.VMEM((n_col, slab, width), f32),
            pltpu.VMEM((slab, cols), f32),
            pltpu.VMEM((n_col, 1, width), f32),
            pltpu.VMEM((1, cols), f32),
            pltpu.VMEM((n_col, 1, width), f32),
            pltpu.VMEM((1, cols), f32),
            pltpu.VMEM((n_col, 1, width), f32),
            pltpu.VMEM((n_col, 1, width), f32),
            pltpu.VMEM((n_col, 1, cols), f32),
            pltpu.VMEM((ITERS, 1, cols), f32),
            pltpu.VMEM((ITERS, n_row, 1, cols), f32),
            pltpu.VMEM((col_blocks, block, width) if exact else (1, 8, 128), f32),
            pltpu.VMEM((8, cols), f32),
            pltpu.VMEM((n_col, 1, 128), f32),
            pltpu.SemaphoreType.DMA((n_col,)),
            pltpu.SemaphoreType.DMA((n_col,)),
            pltpu.SemaphoreType.DMA((n_col,)),
            pltpu.SemaphoreType.DMA((n_col,)),
            pltpu.SemaphoreType.DMA((ITERS, n_row)),
            pltpu.SemaphoreType.DMA((ITERS, n_row)),
            pltpu.SemaphoreType.DMA((n_col,)),
            pltpu.SemaphoreType.DMA((n_col,)),
        ],
        compiler_params=pltpu.CompilerParams(
            collective_id=int(exact), has_side_effects=True, vmem_limit_bytes=56 * 1024 * 1024
        ),
        cost_estimate=pl.CostEstimate(
            flops=2 * 2 * ITERS * pairs * depth,
            bytes_accessed=row_blocks * dim * block * 2,
            transcendentals=2 * ITERS * pairs,
        ),
    )(block_lists, row_points, col_points)


def fast_kernel(
    n_row, n_col, lists_ref, x_ref, y_ref, f_ref, g_ref, flag_ref,
    a_ref, b_ref, bt_ref, abase, bbase, t_ref, u_ref, nx_ref, ny_ref,
    l_ref, rs_recv, c_send, c_recv, sums_ref, flag_recv,
    rs_ssem, rs_rsem, ag_ssem, ag_rsem, c_ssem, c_rsem, flag_ssem, flag_rsem,
):
    me_row = lax.axis_index("row")
    me_col = lax.axis_index("col")
    row_blocks, dim, block = x_ref.shape
    col_blocks = y_ref.shape[0]
    per = row_blocks // n_col
    width = per * block
    cols = col_blocks * block
    log2_a = -math.log2(n_row * row_blocks * block)
    log2_b = -math.log2(n_col * cols)
    alpha = 2.0 * kappa / dim
    beta = kappa / dim
    bias_rows = pl.ds(dim, slab)
    spare_rows = pl.ds(dim + slab, shallow - dim - slab)
    inverse = 1.0 / alpha

    barrier = pltpu.get_barrier_semaphore()
    for step in range(1, n_col):
        pl.semaphore_signal(
            barrier, inc=1, device_id={"col": lax.rem(me_col + step, n_col)}, device_id_type=MESH
        )
    for step in range(1, n_row):
        pl.semaphore_signal(
            barrier, inc=1, device_id={"row": lax.rem(me_row + step, n_row)}, device_id_type=MESH
        )

    slab_rows = lax.broadcasted_iota(jnp.int32, (slab, block), 0)
    zeros = jnp.zeros((shallow - dim - slab, block), jnp.bfloat16)

    for c in range(col_blocks):
        lanes = pl.ds(c * block, block)
        y = y_ref[c]
        b_ref[pl.ds(0, dim), lanes] = y
        y32 = y.astype(jnp.float32)
        norm = jnp.sum(y32 * y32, axis=0, keepdims=True) * beta
        ny_ref[:, lanes] = norm
        u_ref[:, lanes] = -norm
        base = jnp.where((slab_rows < 3) | (slab_rows == 6 + c), 1.0, 0.0)
        bbase[:, lanes] = base
        b_ref[bias_rows, lanes] = with_bias(base, norm * -inverse, 3).astype(jnp.bfloat16)
        b_ref[spare_rows, lanes] = zeros
        bt_ref[pl.ds(c * block, block), :] = b_ref[:, lanes].T

    def prepare(q, carry):
        for i in range(per):
            r = q * per + i
            lanes = pl.ds(i * block, block)
            x = x_ref[r].astype(jnp.float32)
            norm = jnp.sum(x * x, axis=0, keepdims=True) * beta
            nx_ref[q, :, lanes] = norm
            t_ref[q, :, lanes] = -norm
            a_ref[q, pl.ds(0, dim), lanes] = x_ref[r]
            listed = lists_ref[pl.ds(r, 1), :]
            base = jnp.where((slab_rows >= 3) & (slab_rows < 6), 1.0, 0.0)
            for c in range(col_blocks):
                hit = jnp.where(listed == me_col * col_blocks + c, 1.0, 0.0)
                hit = jnp.max(hit, axis=1, keepdims=True)
                fill = jnp.broadcast_to(jnp.where(hit > 0.0, 0.0, masked_score), (slab, block))
                base = jnp.where(slab_rows == 6 + c, fill, base)
            abase[q, :, lanes] = base
            a_ref[q, bias_rows, lanes] = with_bias(base, (lift - norm) * inverse, 0).astype(jnp.bfloat16)
            a_ref[q, spare_rows, lanes] = zeros
        return carry

    lax.fori_loop(0, n_col, prepare, 0)
    pl.semaphore_wait(barrier, n_col - 1 + n_row - 1)

    def scatter_copy(peer):
        return pltpu.make_async_remote_copy(
            src_ref=l_ref.at[peer], dst_ref=rs_recv.at[me_col],
            send_sem=rs_ssem, recv_sem=rs_rsem,
            device_id={"col": peer}, device_id_type=MESH,
        )

    def gather_copy(peer):
        return pltpu.make_async_remote_copy(
            src_ref=t_ref.at[me_col], dst_ref=t_ref.at[me_col],
            send_sem=ag_ssem, recv_sem=ag_rsem,
            device_id={"col": peer}, device_id_type=MESH,
        )

    def col_copy(k, peer):
        return pltpu.make_async_remote_copy(
            src_ref=c_send.at[k], dst_ref=c_recv.at[k, me_row],
            send_sem=c_ssem.at[k], recv_sem=c_rsem.at[k],
            device_id={"row": peer}, device_id_type=MESH,
        )

    def flag_copy(peer):
        return pltpu.make_async_remote_copy(
            src_ref=flag_recv.at[me_col], dst_ref=flag_recv.at[me_col],
            send_sem=flag_ssem, recv_sem=flag_rsem,
            device_id={"col": peer}, device_id_type=MESH,
        )

    def wait_all(ref, peers, sem):
        some = ref.at[pl.ds(0, peers)]
        pltpu.make_async_copy(some, some, sem).wait()

    col_peers = [lax.rem(me_col + step, n_col) for step in range(1, n_col)]
    row_peers = [lax.rem(me_row + step, n_row) for step in range(1, n_row)]

    def exponentials(q, i, c):
        scores = jnp.dot(
            bt_ref[pl.ds(c * block, block), :],
            a_ref[q, :, pl.ds(i * block, block)],
            preferred_element_type=jnp.float32,
        )
        return jnp.exp2(scores * alpha)

    def row_part(q):
        for i in range(per):
            total = jnp.zeros((8, block), jnp.float32)
            for c in range(col_blocks):
                total += jnp.sum(exponentials(q, i, c).reshape(block // 8, 8, block), axis=0)
            l_ref[q, :, pl.ds(i * block, block)] = jnp.sum(total, axis=0, keepdims=True)

    def col_part(q):
        bias = (t_ref[q] + lift) * inverse
        a_ref[q, bias_rows, :] = with_bias(abase[q], bias, 0).astype(jnp.bfloat16)
        for c in range(col_blocks):
            folded = None
            for i in range(per):
                terms = exponentials(q, i, c)
                for j in range(0, block, 128):
                    piece = terms[:, j : j + 128]
                    folded = piece if folded is None else folded + piece
            sums_ref[pl.ds(c * block, block), :] += folded

    def iteration(k, carry):
        def row_step(s, c2):
            q = lax.rem(me_col + 1 + s, n_col)
            row_part(q)
            scatter_copy(q).start()
            return c2

        lax.fori_loop(0, n_col - 1, row_step, 0)
        row_part(me_col)
        rs_recv[me_col] = l_ref[me_col]
        wait_all(rs_recv, n_col - 1, rs_rsem)
        whole = jnp.sum(rs_recv[...], axis=0)
        t_ref[me_col] = t_ref[me_col] + ((log2_a + lift) - lifted_log2(whole))
        for peer in col_peers:
            gather_copy(peer).start()

        sums_ref[...] = jnp.zeros((cols, 128), jnp.float32)
        col_part(me_col)
        wait_all(t_ref, n_col - 1, ag_rsem)

        def col_step(s, c2):
            col_part(lax.rem(me_col + 1 + s, n_col))
            return c2

        lax.fori_loop(0, n_col - 1, col_step, 0)
        share = jnp.sum(sums_ref[...].T, axis=0, keepdims=True)
        c_send[k] = share
        for peer in row_peers:
            col_copy(k, peer).start()
        c_recv[k, me_row] = share
        wait_all(l_ref, n_col - 1, rs_ssem)
        wait_all(t_ref, n_col - 1, ag_ssem)
        wait_all(c_recv.at[k], n_row - 1, c_rsem.at[k])
        whole = jnp.sum(c_recv[k], axis=0)
        u_ref[...] = u_ref[...] + ((log2_b + lift) - lifted_log2(whole))
        b_ref[bias_rows, :] = with_bias(bbase[...], u_ref[...] * inverse, 3).astype(jnp.bfloat16)
        bt_ref[...] = b_ref[...].T
        return carry

    lax.fori_loop(0, ITERS, iteration, 0)

    for q in range(n_col):
        for i in range(per):
            lanes = pl.ds(i * block, block)
            f_ref[pl.ds(q * per + i, 1), :] = (t_ref[q, :, lanes] + nx_ref[q, :, lanes]) * (
                1.0 / kappa
            )
    flag_recv[me_col] = sum(u_ref[:, i * 128 : (i + 1) * 128] for i in range(cols // 128))
    for peer in col_peers:
        flag_copy(peer).start()
    potential = (u_ref[...] + ny_ref[...]) * (1.0 / kappa)
    for c in range(col_blocks):
        g_ref[pl.ds(c, 1), :] = potential[:, c * block : (c + 1) * block]
    for k in range(ITERS):
        wait_all(c_recv.at[k], n_row - 1, c_ssem.at[k])
    wait_all(flag_recv, n_col - 1, flag_rsem)
    wait_all(flag_recv, n_col - 1, flag_ssem)
    seen = jnp.sum(jnp.sum(flag_recv[...], axis=0), axis=1, keepdims=True)
    flag_ref[...] = jnp.broadcast_to(jnp.where(seen == seen, 0, 1), flag_ref.shape)


def run_fast(n_row, n_col, row_points, col_points, block_lists):
    row_blocks, dim, block = row_points.shape
    col_blocks = col_points.shape[0]
    width = row_blocks // n_col * block
    cols = col_blocks * block
    f32, bf16 = jnp.float32, jnp.bfloat16
    pairs = row_blocks * col_blocks * block * block
    vmem = pl.BlockSpec(memory_space=pltpu.VMEM)
    sems = pltpu.SemaphoreType.DMA
    return pl.pallas_call(
        functools.partial(fast_kernel, n_row, n_col),
        out_shape=(
            jax.ShapeDtypeStruct((row_blocks, block), f32),
            jax.ShapeDtypeStruct((col_blocks, block), f32),
            jax.ShapeDtypeStruct((1, 128), jnp.int32),
        ),
        in_specs=[vmem] * 3,
        out_specs=(vmem, vmem, vmem),
        scratch_shapes=[
            pltpu.VMEM((n_col, shallow, width), bf16),
            pltpu.VMEM((shallow, cols), bf16),
            pltpu.VMEM((cols, shallow), bf16),
            pltpu.VMEM((n_col, slab, width), f32),
            pltpu.VMEM((slab, cols), f32),
            pltpu.VMEM((n_col, 1, width), f32),
            pltpu.VMEM((1, cols), f32),
            pltpu.VMEM((n_col, 1, width), f32),
            pltpu.VMEM((1, cols), f32),
            pltpu.VMEM((n_col, 1, width), f32),
            pltpu.VMEM((n_col, 1, width), f32),
            pltpu.VMEM((ITERS, 1, cols), f32),
            pltpu.VMEM((ITERS, n_row, 1, cols), f32),
            pltpu.VMEM((cols, 128), f32),
            pltpu.VMEM((n_col, 1, 128), f32),
            sems, sems, sems, sems,
            sems((ITERS,)), sems((ITERS,)),
            sems, sems,
        ],
        compiler_params=pltpu.CompilerParams(
            collective_id=0, has_side_effects=True, vmem_limit_bytes=40 * 1024 * 1024
        ),
        cost_estimate=pl.CostEstimate(
            flops=2 * 2 * ITERS * pairs * shallow,
            bytes_accessed=row_blocks * dim * block * 2,
            transcendentals=2 * ITERS * pairs,
        ),
    )(block_lists, row_points, col_points)


def body(n_row, n_col, *arguments):
    row_potential, col_potential, flag = run_fast(n_row, n_col, *arguments)
    return lax.cond(
        flag[0, 0] > 0,
        lambda *operands: run(True, n_row, n_col, *operands[2:])[:2],
        lambda *operands: operands[:2],
        row_potential,
        col_potential,
        *arguments,
    )


def solution(mesh):
    placed = (P("row", None, None), P("col", None, None), P("row", None))
    return jax.shard_map(
        functools.partial(body, mesh.shape["row"], mesh.shape["col"]),
        mesh=mesh,
        in_specs=placed,
        out_specs=(P("row", None), P("col", None)),
        check_vma=False,
    )
```
